512 devices in a mesh: seg: 64 (over z, y_lo, core), dom: 8 (over x, y_hi).
Axes of the slice: x: 4, y: 8 (y_hi: 2, y_lo: 4; y = y_hi * 4 + y_lo), z: 8, core: 2. Of those that a mesh axis runs over, the one named last changes fastest.
Arguments:
- tangent: float32 [64, 2, 2048, 512], P('seg', None, 'dom'), may hold values from -6 to 6
- base_swirl: float32 [64, 2048, 512], P('seg', 'dom'), may hold values from -0.5 to 0.5
- metric: float32 [2048, 512], P('dom'), may hold values from 0.05 to 0.2
- stiffness: float32 [8, 8], replicated
- face_slot: int32 [2048, 6], P('dom'), may hold values from 0 to 831, as said below
- corners: int32 [2048, 8], P('dom'), may hold values from 0 to 511
- coarse_inverse: float32 [512, 512], replicated
- phase_angle: float32 [1], replicated, may hold values from -3.140625 to 3.140625
Outputs:
- mismatch: float32 [64, 2, 2048, 512], P('seg', None, 'dom')
The draws below stay inside these ranges and needn't reach their ends.
Inputs may be any that keep to these rules, and one draw needn't show every extreme that they name: `face_slot`: within each slab of 256 elements along dom, every slot from 64 to 767 holds exactly two of the slab's faces, and every slot below 64 or from 768 on holds exactly one.
All inputs are finite; a program needn't handle non-finite values.
Results may differ from the reference program's by a relative error of at most 0.0001.
Values sent between devices are 32-bit elements; how exact they have to be, the bound alone decides.
No kernel may reach another device: no remote copies, remote signals or barrier semaphores. Data moves between devices by JAX's collectives and lax.ppermute only.
A program may use at most 128 MiB of HBM per device.

```python
import math
import jax
import jax.numpy as jnp
import numpy as np
from jax import lax

NP = 8
E_DEV = 256
BFACE = 64
NV = 512
STEPS = 2
ELEMS = 2048
SEGMENTS = 64
N_DOM = 8


def draw_face_slot(key, part):
    key = jax.random.fold_in(key, 11)
    face_count = 6 * E_DEV
    interior = 3 * E_DEV - BFACE

    def draw_block(block_key):
        shuffled = jax.random.permutation(block_key, face_count).astype(jnp.int32)
        paired = BFACE + shuffled // 2
        upstream = shuffled - 2 * interior
        downstream = shuffled - 2 * interior - BFACE + 3 * E_DEV
        chosen = jnp.where(shuffled < 2 * interior, paired, jnp.where(shuffled < 2 * interior + BFACE, upstream, downstream))
        return chosen.reshape(E_DEV, 6)
    dev_keys = jax.random.split(key, ELEMS // E_DEV)
    return jax.vmap(draw_block)(dev_keys).reshape(ELEMS, 6).astype(jnp.int32)


def draw_stiffness(key, part):
    key = jax.random.fold_in(key, 23)
    key_diag, key_off = jax.random.split(key)
    diagonal = jax.random.uniform(key_diag, (NP,), jnp.float32, 0.6, 1.0)
    off_diag = jax.random.normal(key_off, (NP, NP), jnp.float32) * 0.12
    identity = jnp.eye(NP, dtype=jnp.float32)
    return identity * diagonal[:, None] + (1.0 - identity) * off_diag


def draw_coarse_inverse(key, part):
    key = jax.random.fold_in(key, 37)
    key_diag, key_off = jax.random.split(key)
    diagonal = jax.random.uniform(key_diag, (NV,), jnp.float32, 2.0, 4.0)
    off_diag = jax.random.normal(key_off, (NV, NV), jnp.float32) * 2.0 / NV ** 0.5
    identity = jnp.eye(NV, dtype=jnp.float32)
    return identity * diagonal[:, None] + (1.0 - identity) * off_diag


def touch_ends(array, stream_key, low, top_value):
    extent = array.shape
    place = [jax.random.randint(jax.random.fold_in(stream_key, axis), (), 0, extent[axis]) for axis in range(len(extent))]
    array = array.at[tuple(place)].set(low)
    longest = extent.index(max(extent))
    place[longest] = (place[longest] + 1) % extent[longest]
    return array.at[tuple(place)].set(top_value)


def block_scale(stream_key, dims, shards, least, largest):
    def one(dim, shards_of):
        draws = jax.random.uniform(jax.random.fold_in(jax.random.fold_in(stream_key, 6), dim), (shards_of,), jnp.float32, least / len(shards), largest / len(shards))
        return jnp.repeat(jnp.exp(draws), dims[dim] // shards_of).reshape((-1,) + (1,) * (len(dims) - dim - 1))

    level = one(*shards[0])
    for cut in shards[1:]:
        level = level * one(*cut)
    return level


def gaussian(own_key, extent, scale, most, cuts=(), kind=jnp.bfloat16):
    array = jax.random.normal(own_key, extent, jnp.float32) * scale
    if len(cuts) > 0:
        array = block_scale(own_key, extent, cuts, -0.22, 0.18) * array
    return jnp.clip(array, min=-most, max=most).astype(kind)


def setup_inputs(seed: int = 0) -> dict:
    key_of = jax.random.split(jax.random.key(seed), 9)
    tangent = gaussian(key_of[0], (SEGMENTS, 2, ELEMS, NP ** 3), 1.0, 6.0, ((0, 64), (2, 8)), jnp.float32)
    base_swirl = jnp.clip(jax.random.uniform(key_of[1], (SEGMENTS, ELEMS, NP ** 3), jnp.float32, -0.5, 0.5) * block_scale(key_of[1], (SEGMENTS, ELEMS, NP ** 3), ((0, 64), (1, 8)), -0.4, 0.0), -0.5, 0.5)
    metric = jnp.clip(jnp.exp(math.log(0.2) - 1.3862944 * jax.random.uniform(key_of[2], (ELEMS, NP ** 3), jnp.float32) ** block_scale(key_of[2], (ELEMS, NP ** 3), ((0, 8),), -0.2, 0.2)), 0.05, 0.2)
    stiffness = draw_stiffness(jax.random.fold_in(key_of[8], 71), 0)
    face_slot = draw_face_slot(jax.random.fold_in(key_of[8], 71), 0)
    corners = touch_ends(jax.random.randint(key_of[5], (ELEMS, 8), 0, NV), jax.random.fold_in(key_of[5], 1), 0, NV - 1).astype(jnp.int32)
    coarse_inverse = draw_coarse_inverse(jax.random.fold_in(key_of[8], 71), 0)
    phase_angle = jnp.clip(jax.random.uniform(key_of[7], (1,), jnp.float32, -3.140625, 3.140625), -3.140625, 3.140625)
    return dict(tangent=tangent, base_swirl=base_swirl, metric=metric, stiffness=stiffness, face_slot=face_slot, corners=corners, coarse_inverse=coarse_inverse, phase_angle=phase_angle)


def corner_table(edge_nodes):
    points = -np.cos(np.pi * np.arange(edge_nodes) / (edge_nodes - 1))
    linear = np.stack([(1.0 - points) / 2.0, (1.0 + points) / 2.0])
    values_table = linear[:, None, None, :, None, None] * linear[None, :, None, None, :, None] * linear[None, None, :, None, None, :]
    return values_table.reshape(8, edge_nodes ** 3)


def reference(tangent, base_swirl, metric, stiffness, face_slot, corners, coarse_inverse, phase_angle):
    exact_mode = lax.Precision.HIGHEST
    edge_nodes = NP
    node_count = NP ** 3
    interior = 3 * E_DEV - BFACE
    slot_total = N_DOM * BFACE + N_DOM * interior
    owner_dev = (jnp.arange(ELEMS, dtype=jnp.int32) // E_DEV)[:, None]
    upstream = owner_dev * BFACE + face_slot
    paired = N_DOM * BFACE + owner_dev * interior + (face_slot - BFACE)
    downstream = ((owner_dev + 1) % N_DOM) * BFACE + (face_slot - 3 * E_DEV)
    global_slot = jnp.where(face_slot < BFACE, upstream, jnp.where(face_slot >= 3 * E_DEV, downstream, paired)).reshape(-1).astype(jnp.int32)
    basis = jnp.asarray(corner_table(edge_nodes), dtype=jnp.float32)
    corner_flat = corners.reshape(-1).astype(jnp.int32)

    def shoot_step(current, swirl):
        cube_view = current.reshape(2, ELEMS, edge_nodes, edge_nodes, edge_nodes)
        stiff_part = jnp.einsum('ij,cejab->ceiab', stiffness, cube_view, precision=exact_mode)
        stiff_part = stiff_part + jnp.einsum('ij,ceajb->ceaib', stiffness, cube_view, precision=exact_mode)
        stiff_part = stiff_part + jnp.einsum('ij,ceabj->ceabi', stiffness, cube_view, precision=exact_mode)
        stiff_part = stiff_part.reshape(2, ELEMS, node_count)
        turned = jnp.stack([-current[1], current[0]])
        advanced = current - metric[None] * stiff_part + swirl[None] * turned
        cube_view = advanced.reshape(2, ELEMS, edge_nodes, edge_nodes, edge_nodes)
        face_vals = jnp.stack([cube_view[:, :, 0], cube_view[:, :, -1], cube_view[:, :, :, 0], cube_view[:, :, :, -1], cube_view[:, :, :, :, 0], cube_view[:, :, :, :, -1]], axis=2)
        flat_faces = face_vals.reshape(2, ELEMS * 6, edge_nodes * edge_nodes)
        slot_sums = jax.ops.segment_sum(jnp.transpose(flat_faces, (1, 0, 2)), global_slot, num_segments=slot_total)
        gathered_back = jnp.transpose(slot_sums[global_slot], (1, 0, 2))
        lift_vals = (0.5 * gathered_back - flat_faces).reshape(2, ELEMS, 6, edge_nodes, edge_nodes)
        cube_view = cube_view.at[:, :, 0].add(lift_vals[:, :, 0])
        cube_view = cube_view.at[:, :, -1].add(lift_vals[:, :, 1])
        cube_view = cube_view.at[:, :, :, 0].add(lift_vals[:, :, 2])
        cube_view = cube_view.at[:, :, :, -1].add(lift_vals[:, :, 3])
        cube_view = cube_view.at[:, :, :, :, 0].add(lift_vals[:, :, 4])
        cube_view = cube_view.at[:, :, :, :, -1].add(lift_vals[:, :, 5])
        settled = cube_view.reshape(2, ELEMS, node_count)
        restricted = jnp.einsum('cen,kn->cek', settled, basis, precision=exact_mode) / node_count
        coarse = jax.ops.segment_sum(restricted.reshape(2, ELEMS * 8).T, corner_flat, num_segments=NV).T
        solved = jnp.dot(coarse, coarse_inverse.T, precision=exact_mode)
        spread = solved[:, corner_flat].reshape(2, ELEMS, 8)
        correction = jnp.einsum('cek,kn->cen', spread, basis, precision=exact_mode)
        return settled - correction

    def shoot(pair):
        current, swirl = pair
        for step_num in range(STEPS):
            current = shoot_step(current, swirl)
        return current

    end_state = lax.map(shoot, (tangent, base_swirl))
    arrived = jnp.roll(end_state, 1, axis=0)
    angles = jnp.where(jnp.arange(SEGMENTS) == 0, phase_angle[0], jnp.zeros((), jnp.float32))
    cosine = jnp.cos(angles)[:, None, None]
    sine = jnp.sin(angles)[:, None, None]
    rotated = jnp.stack([cosine * arrived[:, 0] - sine * arrived[:, 1], sine * arrived[:, 0] + cosine * arrived[:, 1]], axis=1)
    return tangent - rotated
```

```python
import jax
import jax.numpy as jnp
import numpy as np
from jax import lax
from jax.experimental import pallas as pl
from jax.experimental.pallas import tpu as pltpu
from jax.sharding import PartitionSpec as P

F32 = jnp.float32
BF16 = jnp.bfloat16
NP = 8
NODES = 512
ELEMS = 256
FACES = 6
PLANE = 64
SHARED = 64
HALO = 2 * SHARED
INNER_TOP = 768
MSG1 = 88
MSG2 = 72
FACE_CORNERS = (
    (0, 1, 2, 3),
    (4, 5, 6, 7),
    (0, 1, 4, 5),
    (2, 3, 6, 7),
    (0, 2, 4, 6),
    (1, 3, 5, 7),
)


def tables():
    points = -np.cos(np.pi * np.arange(NP) / (NP - 1))
    linear = np.stack([(1.0 - points) / 2.0, (1.0 + points) / 2.0])
    basis = (
        linear[:, None, None, :, None, None]
        * linear[None, :, None, None, :, None]
        * linear[None, None, :, None, None, :]
    ).reshape(8, NODES)
    flat = (linear[:, None, :, None] * linear[None, :, None, :]).reshape(4, PLANE)
    pair = np.zeros((8, 2 * PLANE))
    pair[:4, :PLANE] = flat
    pair[4:, PLANE:] = flat
    node = np.arange(NODES).reshape(NP, NP, NP)
    faces = [node[0], node[-1], node[:, 0], node[:, -1], node[:, :, 0], node[:, :, -1]]
    chosen = np.concatenate([f.reshape(-1) for f in faces])
    select = (np.arange(NODES)[:, None] == chosen[None, :]).astype(np.float32)
    return basis.astype(np.float32), pair.astype(np.float32), select


def dot(a, b):
    return lax.dot_general(a, b, (((1,), (0,)), ((), ())), preferred_element_type=F32)


def dot_nt(a, b):
    return lax.dot_general(a, b, (((1,), (1,)), ((), ())), preferred_element_type=F32)


def dot_tn(a, b):
    return lax.dot_general(a, b, (((0,), (0,)), ((), ())), preferred_element_type=F32)


def split(x):
    high = x.astype(BF16)
    return high, (x - high.astype(F32)).astype(BF16)


def stacked(x):
    high = x.astype(BF16).astype(F32)
    return jnp.concatenate([high, x - high], axis=0).astype(BF16)


def hot(mask):
    return jnp.where(mask, F32(1.0), F32(0.0)).astype(BF16)


def iota(shape, dim):
    return lax.broadcasted_iota(jnp.int32, shape, dim)


def slot_rows(fs_ref):
    rows = fs_ref[...].astype(F32)
    return [rows[f : f + 1, :] for f in range(FACES)]


def slot_columns(fs_ref):
    rows = fs_ref[...].astype(F32)
    columns = jnp.concatenate([rows, rows[:2]], axis=0).T
    return [columns[:, f : f + 1] for f in range(FACES)]


def corner_parts(cor_ref):
    ids = cor_ref[...]
    return (ids >> 7).astype(F32), (ids & 127).astype(F32)


def row_of(parts):
    return jnp.concatenate([parts[k : k + 1, :] for k in range(parts.shape[0])], axis=1)


def stiff_matrix(sti):
    rest = sti - sti.astype(BF16).astype(F32)
    low = rest - rest.astype(BF16).astype(F32)
    parts = jnp.concatenate(
        [sti.astype(BF16).astype(F32), rest.astype(BF16).astype(F32), low, jnp.zeros((8, 8), F32)], axis=0
    ).astype(BF16)
    row, col = iota((NODES, 8), 0), iota((NODES, 8), 1)
    col32, lane = iota((32, NODES), 0), iota((32, NODES), 1)
    from_n = iota((NODES, 1), 0)
    to_n = iota((1, NODES), 1)
    total = jnp.zeros((NODES, NODES), F32)
    for shift, keep in ((6, 63), (3, 455), (0, 504)):
        source = hot(((row >> shift) & 7) == col)
        target = hot(((lane >> shift) & 7) == (col32 & 7))
        spread = dot_nt(source, parts)
        spread = dot(spread.astype(BF16), target)
        same = (from_n & keep) == (to_n & keep)
        total = total + jnp.where(same, spread, F32(0.0))
    return total


def advance(state, bh, bl, metric, swirl):
    high, low = split(state)
    stiff = dot(high, bh) + dot(low, bh) + dot(high, bl)
    re, im = state[:ELEMS], state[ELEMS:]
    new_re = re - metric * stiff[:ELEMS] - swirl * im
    new_im = im - metric * stiff[ELEMS:] + swirl * re
    return jnp.concatenate([new_re, new_im], axis=0)


def face_block(fh, fl, f):
    lanes = slice(f * PLANE, (f + 1) * PLANE)
    return jnp.concatenate(
        [fh[:ELEMS, lanes], fh[ELEMS:, lanes], fl[:ELEMS, lanes], fl[ELEMS:, lanes]], axis=1
    ).astype(BF16)


def to_elements(blocks):
    re = jnp.concatenate([b[:, :PLANE] for b in blocks], axis=1)
    im = jnp.concatenate([b[:, PLANE:] for b in blocks], axis=1)
    return jnp.concatenate([re, im], axis=0)


def multiplicity():
    n = iota((1, NODES), 1)
    total = jnp.zeros((1, NODES), F32)
    for shift in (6, 3, 0):
        at = (n >> shift) & 7
        total = total + jnp.where((at == 0) | (at == 7), F32(1.0), F32(0.0))
    return total


def deposit(values, high_ids, low_hot):
    vh = (iota((8, 1), 0) & 3).astype(F32)
    chosen = jnp.where(high_ids == vh, values, F32(0.0))
    both = dot_nt(stacked(chosen), low_hot)
    return both[:8] + both[8:]


def eight(re, im):
    return jnp.where(iota((8, 1), 0) < 4, re, im)


def coarse_of(settled, basis, cvh_row, bm):
    sh, sl = split(settled)
    scaled = basis * F32(1.0 / NODES)
    two = stacked(scaled)
    first = dot_nt(two, sh)
    second = dot_nt(two, sl)
    r = first[:8] + first[8:] + second[:8]
    re = row_of(r[:, :ELEMS])
    im = row_of(r[:, ELEMS:])
    return deposit(eight(re, im), cvh_row, bm)


def face_restricted(yh, yl, pair):
    scaled = pair * F32(0.5 / NODES)
    two = stacked(scaled)
    first = dot_nt(two, yh.astype(BF16))
    second = dot_nt(two, yl.astype(BF16))
    return first[:8] + first[8:] + second[:8]


def solve(coarse, kh, kl):
    rows = [jnp.concatenate([coarse[4 * c + h : 4 * c + h + 1] for h in range(4)], axis=1) for c in range(2)]
    flat = jnp.concatenate(rows, axis=0)
    high = flat.astype(BF16).astype(F32)
    packed = jnp.concatenate([high, flat - high, jnp.zeros((12, NODES), F32)], axis=0).astype(BF16)
    first = dot_nt(packed, kh)
    second = dot_nt(packed, kl)
    solved = first[0:2] + first[2:4] + second[0:2]
    return jnp.concatenate(
        [solved[c : c + 1, 128 * h : 128 * (h + 1)] for c in range(2) for h in range(4)], axis=0
    )


def correction(solved, basis, cvh_row, bm):
    both = dot(stacked(solved), bm)
    spread = both[:8] + both[8:]
    vh = (iota((8, 1), 0) & 3).astype(F32)
    spread = jnp.where(cvh_row == vh, spread, F32(0.0))
    lines = []
    for c in range(2):
        line = jnp.sum(spread[4 * c : 4 * c + 4], axis=0, keepdims=True)
        lines.append(jnp.concatenate([line[:, ELEMS * k : ELEMS * (k + 1)] for k in range(8)], axis=0))
    by_corner = jnp.concatenate(lines, axis=1)
    high = by_corner.astype(BF16).astype(F32)
    left = jnp.concatenate([high, by_corner - high, high, jnp.zeros((8, NODES), F32)], axis=0)
    bas_high = basis.astype(BF16).astype(F32)
    right = jnp.concatenate([bas_high, bas_high, basis - bas_high, jnp.zeros((8, NODES), F32)], axis=0)
    return dot_tn(left.astype(BF16), right.astype(BF16))


def shared_target_column():
    s = iota((HALO, 1), 0)
    return jnp.where(s < SHARED, s, s + (INNER_TOP - SHARED)).astype(F32)


def shared_target_row():
    s = iota((1, HALO), 1)
    return jnp.where(s < SHARED, s, s + (INNER_TOP - SHARED)).astype(F32)


def halo_part(columns, arrived, select):
    high, low = split(arrived)
    both = jnp.concatenate([high.astype(F32), low.astype(F32)], axis=1).astype(BF16)
    target = shared_target_row()
    blocks_h, blocks_l = [], []
    for f in range(FACES):
        got = dot(hot(columns[f] == target), both)
        blocks_h.append(got[:, :HALO])
        blocks_l.append(got[:, HALO:])
    return dot_nt(to_elements(blocks_h).astype(BF16), select) + dot_nt(
        to_elements(blocks_l).astype(BF16), select
    )


def local_settle(advanced, select, pairing, q_ref, out_ref):
    ah, al = split(advanced)
    fh = dot(ah, select)
    fl = dot(al, select)
    for f in range(FACES):
        q_ref[f * ELEMS : (f + 1) * ELEMS, :] = face_block(fh, fl, f)
    blocks = []
    for f in range(FACES):
        got = dot(pairing(f), q_ref[...])
        blocks.append(got[:, :HALO] + got[:, HALO:])
    gathered = to_elements(blocks)
    gh, gl = split(gathered)
    lift = dot_nt(gh, select) + dot_nt(gl, select)
    out_ref[...] = advanced * (F32(1.0) - multiplicity()) + F32(0.5) * lift


def send_rows(msg_ref, me, head, rows):
    count = head.shape[0]
    up, down = rows[:SHARED], rows[SHARED:]
    after = lax.rem(me + 1, 8)
    for j in range(8):
        msg_ref[j, 0:count, :] = head
        msg_ref[j, count : count + SHARED, :] = jnp.where(after == j, down, up)


def first_kernel(
    tan_ref, swl_ref, met_ref, sti_ref, fs_ref, cor_ref, sel_ref, bas_ref, pair_ref,
    out_ref, msg_ref, p_ref, bm_ref, bh_ref, bl_ref, q_ref,
):
    me = lax.axis_index("dom")
    bh, bl = split(stiff_matrix(sti_ref[...]))
    bh_ref[...] = bh
    bl_ref[...] = bl
    rows = slot_rows(fs_ref)
    row = jnp.concatenate(rows, axis=1)
    columns = slot_columns(fs_ref)
    for f in range(FACES):
        p_ref[f * ELEMS : (f + 1) * ELEMS, :] = hot(columns[f] == row)
    cvh, cvl = corner_parts(cor_ref)
    cvh_row = row_of(cvh)
    bm_ref[...] = hot(row_of(cvl) == iota((128, 1), 0).astype(F32))
    basis = bas_ref[...]

    advanced = advance(tan_ref[...], bh_ref[...], bl_ref[...], met_ref[...], swl_ref[...])
    local_settle(
        advanced, sel_ref[...], lambda f: p_ref[f * ELEMS : (f + 1) * ELEMS, :], q_ref, out_ref
    )
    coarse = coarse_of(out_ref[...], basis, cvh_row, bm_ref[...])
    shared = hot(shared_target_column() == row)
    y = dot(shared, q_ref[...])
    yh, yl = y[:, :HALO], y[:, HALO:]
    rf = face_restricted(yh, yl, pair_ref[...])
    face_ids = jnp.concatenate(
        [
            jnp.concatenate(
                [part[FACE_CORNERS[f][r] : FACE_CORNERS[f][r] + 1, :] for f in range(FACES)], axis=1
            )
            for part in (cvh, cvl)
            for r in range(4)
        ]
        * 2,
        axis=0,
    ).astype(BF16)
    ids = dot_nt(face_ids, shared)[:8]
    send_rows(msg_ref, me, jnp.concatenate([coarse, rf, ids], axis=0), yh + yl)


def second_kernel(
    s1_ref, got_ref, p_ref, bm_ref, bh_ref, bl_ref, swl_ref, met_ref, fs_ref, cor_ref, sel_ref, bas_ref,
    pair_ref, inv_ref,
    out_ref, msg_ref, q_ref,
):
    me = lax.axis_index("dom")
    before, after = lax.rem(me + 7, 8), lax.rem(me + 1, 8)
    kh, kl = split(inv_ref[...])
    basis = bas_ref[...]
    select = sel_ref[...]
    columns = slot_columns(fs_ref)
    row = jnp.concatenate(slot_rows(fs_ref), axis=1)
    cvh, _ = corner_parts(cor_ref)
    cvh_row = row_of(cvh)
    which = iota((128, 1), 0).astype(F32)

    coarse = got_ref[0, 0:8, :]
    for j in range(1, 8):
        coarse = coarse + got_ref[j, 0:8, :]
    rf = jnp.concatenate([got_ref[j, 8:16, :] for j in range(8)], axis=1)
    ids = jnp.concatenate([got_ref[j, 16:24, :] for j in range(8)], axis=1)
    from_left = jnp.concatenate([ids[:, 1024 - SHARED :], ids[:, : 1024 - SHARED]], axis=1)
    from_right = jnp.concatenate([ids[:, SHARED:], ids[:, :SHARED]], axis=1)
    partner = jnp.where((iota((1, 1024), 1) & SHARED) == 0, from_left, from_right)
    for r in range(4):
        low_hot = hot(partner[4 + r : 5 + r, :] == which)
        coarse = coarse + deposit(
            eight(rf[r : r + 1, :], rf[4 + r : 5 + r, :]), partner[r : r + 1, :], low_hot
        )
    solved = solve(coarse, kh, kl)

    arrived = jnp.concatenate([got_ref[before, 24:MSG1, :], got_ref[after, 24:MSG1, :]], axis=0)
    current = (
        s1_ref[...]
        + F32(0.5) * halo_part(columns, arrived, select)
        - correction(solved, basis, cvh_row, bm_ref[...])
    )
    advanced = advance(current, bh_ref[...], bl_ref[...], met_ref[...], swl_ref[...])
    local_settle(advanced, select, lambda f: p_ref[f * ELEMS : (f + 1) * ELEMS, :], q_ref, out_ref)
    coarse = coarse_of(out_ref[...], basis, cvh_row, bm_ref[...])
    shared = hot(shared_target_column() == row)
    y = dot(shared, q_ref[...])
    yh, yl = y[:, :HALO], y[:, HALO:]
    rf = face_restricted(yh, yl, pair_ref[...])
    mine = jnp.concatenate([got_ref[before, 16:24, SHARED:], got_ref[after, 16:24, :SHARED]], axis=1)
    for r in range(4):
        low_hot = hot(mine[4 + r : 5 + r, :] == which)
        coarse = coarse + deposit(eight(rf[r : r + 1, :], rf[4 + r : 5 + r, :]), mine[r : r + 1, :], low_hot)
    send_rows(msg_ref, me, coarse, yh + yl)


def pack_kernel(got_ref, inv_ref, out_ref):
    me = lax.axis_index("dom")
    kh, kl = split(inv_ref[...])
    coarse = got_ref[0, 0:8, :]
    for j in range(1, 8):
        coarse = coarse + got_ref[j, 0:8, :]
    out_ref[0:8, :] = solve(coarse, kh, kl)
    out_ref[8 : 8 + SHARED, :] = got_ref[lax.rem(me + 7, 8), 8:MSG2, :]
    out_ref[8 + SHARED :, :] = got_ref[lax.rem(me + 1, 8), 8:MSG2, :]


def last_kernel(tan_ref, s2_ref, small_ref, bm_ref, fs_ref, cor_ref, sel_ref, bas_ref, ang_ref, out_ref):
    cvh, _ = corner_parts(cor_ref)
    state = (
        s2_ref[...]
        + F32(0.5) * halo_part(slot_columns(fs_ref), small_ref[8:, :], sel_ref[...])
        - correction(small_ref[0:8, :], bas_ref[...], row_of(cvh), bm_ref[...])
    )
    angle = jnp.where(lax.axis_index("seg") == 0, ang_ref[0], F32(0.0))
    angles = jnp.full((1, NODES), angle, F32)
    cosine, sine = jnp.cos(angles), jnp.sin(angles)
    re, im = state[:ELEMS], state[ELEMS:]
    out_ref[0:ELEMS, :] = tan_ref[0:ELEMS, :] - (cosine * re - sine * im)
    out_ref[ELEMS:, :] = tan_ref[ELEMS:, :] - (sine * re + cosine * im)


VMEM = pl.BlockSpec(memory_space=pltpu.VMEM)
SMEM = pl.BlockSpec(memory_space=pltpu.SMEM)


def call(body, outs, scratch, ins, flops, specs=None, limit=40):
    size = sum(int(np.prod(o.shape)) * o.dtype.itemsize for o in outs)
    size += sum(int(np.prod(a.shape)) * a.dtype.itemsize for a in ins)
    return pl.pallas_call(
        body,
        out_shape=outs,
        in_specs=specs or [VMEM] * len(ins),
        out_specs=[VMEM] * len(outs),
        scratch_shapes=scratch,
        compiler_params=pltpu.CompilerParams(vmem_limit_bytes=limit * 1024 * 1024),
        cost_estimate=pl.CostEstimate(flops=flops, bytes_accessed=size, transcendentals=0),
    )(*ins)


def shards(tangent, base_swirl, metric, stiffness, face_slot, corners, coarse_inverse, phase_angle):
    basis, pair, select = tables()
    basis, pair, select = jnp.asarray(basis), jnp.asarray(pair), jnp.asarray(select, dtype=BF16)
    state = tangent.reshape(2 * ELEMS, NODES)
    swirl = base_swirl.reshape(ELEMS, NODES)
    slots = face_slot.T
    ids = corners.T
    field = jax.ShapeDtypeStruct((2 * ELEMS, NODES), F32)
    square = jax.ShapeDtypeStruct((NODES, NODES), BF16)
    faces = pltpu.VMEM((FACES * ELEMS, 2 * HALO), BF16)

    s1, msg, p, bm, bh, bl = call(
        first_kernel,
        [
            field,
            jax.ShapeDtypeStruct((8, MSG1, 128), F32),
            jax.ShapeDtypeStruct((FACES * ELEMS, FACES * ELEMS), BF16),
            jax.ShapeDtypeStruct((128, 8 * ELEMS), BF16),
            square,
            square,
        ],
        [faces],
        [state, swirl, metric, stiffness, slots, ids, select, basis, pair],
        4_000_000_000,
    )
    got = lax.all_to_all(msg, "dom", 0, 0)
    s2, msg = call(
        second_kernel,
        [field, jax.ShapeDtypeStruct((8, MSG2, 128), F32)],
        [faces],
        [s1, got, p, bm, bh, bl, swirl, metric, slots, ids, select, basis, pair, coarse_inverse],
        4_000_000_000,
    )
    size = lax.axis_size("seg")
    ring = [(i, (i + 1) % size) for i in range(size)]
    s2 = lax.ppermute(s2, "seg", ring)
    got = lax.all_to_all(msg, "dom", 0, 0)
    (small,) = call(
        pack_kernel,
        [jax.ShapeDtypeStruct((8 + HALO, 128), F32)],
        [],
        [got, coarse_inverse],
        100_000_000,
    )
    small = lax.ppermute(small, "seg", ring)
    (out,) = call(
        last_kernel,
        [field],
        [],
        [state, s2, small, bm, slots, ids, select, basis, phase_angle],
        1_000_000_000,
        [VMEM] * 8 + [SMEM],
    )
    return out.reshape(1, 2, ELEMS, NODES)


def solution(mesh):
    return jax.shard_map(
        shards,
        mesh=mesh,
        in_specs=(
            P("seg", None, "dom", None),
            P("seg", "dom", None),
            P("dom", None),
            P(),
            P("dom", None),
            P("dom", None),
            P(),
            P(),
        ),
        out_specs=P("seg", None, "dom", None),
        check_vma=False,
    )
```

```python
import jax
import jax.numpy as jnp
import numpy as np
from jax import lax
from jax.experimental import pallas as pl
from jax.experimental.pallas import tpu as pltpu
from jax.sharding import PartitionSpec as P

F32 = jnp.float32
BF16 = jnp.bfloat16
NP = 8
NODES = 512
ELEMS = 256
FACES = 6
PLANE = 64
SHARED = 64
HALO = 2 * SHARED
INNER_TOP = 768
MSG1 = 88
MSG2 = 72
FACE_CORNERS = (
    (0, 1, 2, 3),
    (4, 5, 6, 7),
    (0, 1, 4, 5),
    (2, 3, 6, 7),
    (0, 2, 4, 6),
    (1, 3, 5, 7),
)


def tables():
    points = -np.cos(np.pi * np.arange(NP) / (NP - 1))
    linear = np.stack([(1.0 - points) / 2.0, (1.0 + points) / 2.0])
    basis = (
        linear[:, None, None, :, None, None]
        * linear[None, :, None, None, :, None]
        * linear[None, None, :, None, None, :]
    ).reshape(8, NODES)
    flat = (linear[:, None, :, None] * linear[None, :, None, :]).reshape(4, PLANE)
    pair = np.zeros((8, 2 * PLANE))
    pair[:4, :PLANE] = flat
    pair[4:, PLANE:] = flat
    node = np.arange(NODES).reshape(NP, NP, NP)
    faces = [node[:, 0], node[:, -1], node[:, :, 0], node[:, :, -1]]
    chosen = np.concatenate([f.reshape(-1) for f in faces])
    select = (np.arange(NODES)[:, None] == chosen[None, :]).astype(np.float32)
    return basis.astype(np.float32), pair.astype(np.float32), select


def dot(a, b):
    return lax.dot_general(a, b, (((1,), (0,)), ((), ())), preferred_element_type=F32)


def dot_nt(a, b):
    return lax.dot_general(a, b, (((1,), (1,)), ((), ())), preferred_element_type=F32)


def dot_tn(a, b):
    return lax.dot_general(a, b, (((0,), (0,)), ((), ())), preferred_element_type=F32)


def split(x):
    high = x.astype(BF16)
    return high, (x - high.astype(F32)).astype(BF16)


def stacked(x):
    high = x.astype(BF16).astype(F32)
    return jnp.concatenate([high, x - high], axis=0).astype(BF16)


def hot(mask):
    return jnp.where(mask, F32(1.0), F32(0.0)).astype(BF16)


def iota(shape, dim):
    return lax.broadcasted_iota(jnp.int32, shape, dim)


def slot_rows(fs_ref):
    rows = fs_ref[...].astype(F32)
    return [rows[f : f + 1, :] for f in range(FACES)]


def slot_columns(fs_ref):
    rows = fs_ref[...].astype(F32)
    columns = jnp.concatenate([rows, rows[:2]], axis=0).T
    return [columns[:, f : f + 1] for f in range(FACES)]


def corner_parts(cor_ref):
    ids = cor_ref[...]
    return (ids >> 7).astype(F32), (ids & 127).astype(F32)


def row_of(parts):
    return jnp.concatenate([parts[k : k + 1, :] for k in range(parts.shape[0])], axis=1)


def stiff_of(state, bh, bl):
    high, low = split(state)
    return dot(high, bh) + dot(low, bh) + dot(high, bl)


def stiff_matrix(sti):
    rest = sti - sti.astype(BF16).astype(F32)
    low = rest - rest.astype(BF16).astype(F32)
    parts = jnp.concatenate(
        [sti.astype(BF16).astype(F32), rest.astype(BF16).astype(F32), low, jnp.zeros((8, 8), F32)], axis=0
    ).astype(BF16)
    row, col = iota((NODES, 8), 0), iota((NODES, 8), 1)
    col32, lane = iota((32, NODES), 0), iota((32, NODES), 1)
    from_n = iota((NODES, 1), 0)
    to_n = iota((1, NODES), 1)
    total = jnp.zeros((NODES, NODES), F32)
    for shift, keep in ((6, 63), (3, 455), (0, 504)):
        source = hot(((row >> shift) & 7) == col)
        target = hot(((lane >> shift) & 7) == (col32 & 7))
        spread = dot_nt(source, parts)
        spread = dot(spread.astype(BF16), target)
        same = (from_n & keep) == (to_n & keep)
        total = total + jnp.where(same, spread, F32(0.0))
    return total


def advance(state, stiff, metric, swirl):
    re, im = state[:ELEMS], state[ELEMS:]
    new_re = re - metric * stiff[:ELEMS] - swirl * im
    new_im = im - metric * stiff[ELEMS:] + swirl * re
    return jnp.concatenate([new_re, new_im], axis=0)


def face_blocks(advanced, select):
    ah, al = split(advanced)
    fh, fl = dot(ah, select), dot(al, select)
    high, low = ah.astype(F32), al.astype(F32)
    ends = (slice(0, PLANE), slice(NODES - PLANE, NODES))
    pairs = [(high[:, lanes], low[:, lanes]) for lanes in ends]
    for f in range(4):
        lanes = slice(f * PLANE, (f + 1) * PLANE)
        pairs.append((fh[:, lanes], fl[:, lanes]))
    blocks = [
        jnp.concatenate([h[:ELEMS], h[ELEMS:], l[:ELEMS], l[ELEMS:]], axis=1).astype(BF16) for h, l in pairs
    ]
    return blocks, ah, al


def scattered(blocks, select):
    def element_rows(faces, offset):
        re = jnp.concatenate([b[:, offset : offset + PLANE] for b in faces], axis=1)
        im = jnp.concatenate([b[:, offset + PLANE : offset + 2 * PLANE] for b in faces], axis=1)
        return jnp.concatenate([re, im], axis=0)

    high = element_rows(blocks[2:], 0).astype(BF16)
    low = element_rows(blocks[2:], HALO).astype(BF16)
    inner = dot_nt(high, select) + dot_nt(low, select)
    ends = []
    for block in blocks[:2]:
        both = block[:, :HALO] + block[:, HALO:]
        ends.append(jnp.concatenate([both[:, :PLANE], both[:, PLANE:]], axis=0))
    gap = jnp.zeros((2 * ELEMS, NODES - 2 * PLANE), F32)
    return inner + jnp.concatenate([ends[0], gap, ends[1]], axis=1)


def multiplicity():
    n = iota((1, NODES), 1)
    total = jnp.zeros((1, NODES), F32)
    for shift in (6, 3, 0):
        at = (n >> shift) & 7
        total = total + jnp.where((at == 0) | (at == 7), F32(1.0), F32(0.0))
    return total


def deposit(values, high_ids, low_hot):
    vh = (iota((8, 1), 0) & 3).astype(F32)
    chosen = jnp.where(high_ids == vh, values, F32(0.0))
    both = dot_nt(stacked(chosen), low_hot)
    return both[:8] + both[8:]


def eight(re, im):
    return jnp.where(iota((8, 1), 0) < 4, re, im)


def two_products(table, high, low):
    first = dot_nt(stacked(table), high)
    second = dot_nt(stacked(table), low)
    return first[:8] + first[8:] + second[:8]


def coarse_of(ah, al, partner, basis, pair, cvh, bm):
    own = two_products(basis * ((F32(1.0) - F32(0.5) * multiplicity()) * F32(1.0 / NODES)), ah, al)
    lifted = two_products(pair * F32(0.5 / NODES), partner[:, :HALO], partner[:, HALO:])
    values = []
    for k in range(8):
        total = eight(own[k : k + 1, :ELEMS], own[k : k + 1, ELEMS:])
        for f in range(FACES):
            if k in FACE_CORNERS[f]:
                r = FACE_CORNERS[f].index(k)
                lanes = slice(f * ELEMS, (f + 1) * ELEMS)
                total = total + eight(lifted[r : r + 1, lanes], lifted[4 + r : 5 + r, lanes])
        values.append(total)
    return deposit(jnp.concatenate(values, axis=1), row_of(cvh), bm)


def solve(coarse, kh, kl):
    rows = [jnp.concatenate([coarse[4 * c + h : 4 * c + h + 1] for h in range(4)], axis=1) for c in range(2)]
    flat = jnp.concatenate(rows, axis=0)
    high = flat.astype(BF16).astype(F32)
    packed = jnp.concatenate([high, flat - high, jnp.zeros((12, NODES), F32)], axis=0).astype(BF16)
    first = dot_nt(packed, kh)
    second = dot_nt(packed, kl)
    solved = first[0:2] + first[2:4] + second[0:2]
    return jnp.concatenate(
        [solved[c : c + 1, 128 * h : 128 * (h + 1)] for c in range(2) for h in range(4)], axis=0
    )


def corner_values(solved, cvh_row, bm):
    both = dot(stacked(solved), bm)
    spread = both[:8] + both[8:]
    vh = (iota((8, 1), 0) & 3).astype(F32)
    spread = jnp.where(cvh_row == vh, spread, F32(0.0))
    lines = []
    for c in range(2):
        line = jnp.sum(spread[4 * c : 4 * c + 4], axis=0, keepdims=True)
        lines.append(jnp.concatenate([line[:, ELEMS * k : ELEMS * (k + 1)] for k in range(8)], axis=0))
    by_corner = jnp.concatenate(lines, axis=1)
    high = by_corner.astype(BF16).astype(F32)
    return jnp.concatenate([high, by_corner - high, high, jnp.zeros((8, NODES), F32)], axis=0).astype(BF16)


def tripled(table):
    high = table.astype(BF16).astype(F32)
    return jnp.concatenate([high, high, table - high, jnp.zeros_like(high)], axis=0).astype(BF16)


def shared_target_column():
    s = iota((HALO, 1), 0)
    return jnp.where(s < SHARED, s, s + (INNER_TOP - SHARED)).astype(F32)


def shared_target_row():
    s = iota((1, HALO), 1)
    return jnp.where(s < SHARED, s, s + (INNER_TOP - SHARED)).astype(F32)


def halo_part(placed, arrived, select):
    high, low = split(arrived)
    both = jnp.concatenate([high.astype(F32), low.astype(F32)], axis=1).astype(BF16)
    got = dot(placed, both)
    return scattered([got[f * ELEMS : (f + 1) * ELEMS] for f in range(FACES)], select)


def settle(advanced, partner, select):
    blocks = [partner[f * ELEMS : (f + 1) * ELEMS].astype(F32) for f in range(FACES)]
    kept = advanced * (F32(1.0) - F32(0.5) * multiplicity())
    return kept + F32(0.5) * scattered(blocks, select)


def pair_up(blocks, p_ref, q_ref, g_ref):
    for f in range(FACES):
        q_ref[f * ELEMS : (f + 1) * ELEMS, :] = blocks[f]
    for f in range(FACES):
        rows = slice(f * ELEMS, (f + 1) * ELEMS)
        g_ref[rows, :] = dot(p_ref[rows, :], q_ref[...]).astype(BF16)


def send_rows(msg_ref, me, head, rows):
    count = head.shape[0]
    up, down = rows[:SHARED], rows[SHARED:]
    after = lax.rem(me + 1, 8)
    for j in range(8):
        msg_ref[j, 0:count, :] = head
        msg_ref[j, count : count + SHARED, :] = jnp.where(after == j, down, up)


def first_kernel(
    tan_hbm, swl_hbm, met_hbm, sti_hbm, fs_hbm, cor_hbm, sel_hbm, bas_hbm, pair_hbm, inv_hbm,
    out_ref, msg_ref, p_ref, bm_ref, bh_ref, bl_ref, kh_ref, kl_ref, pl_ref, lb_ref,
    q_ref, g_ref, tan_ref, swl_ref, met_ref, sti_ref, fs_ref, cor_ref, sel_ref, bas_ref, pair_ref, inv_ref, sems,
):
    me = lax.axis_index("dom")
    moves = [
        pltpu.make_async_copy(src, dst, sems.at[i])
        for i, (src, dst) in enumerate(
            (
                (sti_hbm, sti_ref),
                (fs_hbm, fs_ref),
                (cor_hbm, cor_ref),
                (tan_hbm, tan_ref),
                (met_hbm, met_ref),
                (swl_hbm, swl_ref),
                (sel_hbm, sel_ref),
                (bas_hbm, bas_ref),
                (pair_hbm, pair_ref),
                (inv_hbm, inv_ref),
            )
        )
    ]
    for move in moves:
        move.start()
    for move in moves[:3]:
        move.wait()
    bh, bl = split(stiff_matrix(sti_ref[...]))
    bh_ref[...] = bh
    bl_ref[...] = bl
    rows = slot_rows(fs_ref)
    columns = slot_columns(fs_ref)
    other = iota((ELEMS, 1), 0) != iota((1, ELEMS), 1)
    for f in range(FACES):
        for g in range(FACES):
            same = columns[f] == rows[g]
            if f == g:
                same = same & other
            p_ref[f * ELEMS : (f + 1) * ELEMS, g * ELEMS : (g + 1) * ELEMS] = hot(same)
    cvh, cvl = corner_parts(cor_ref)
    bm_ref[...] = hot(row_of(cvl) == iota((128, 1), 0).astype(F32))
    shared = hot(shared_target_column() == jnp.concatenate(rows, axis=1))
    face_ids = jnp.concatenate(
        [
            jnp.concatenate(
                [part[FACE_CORNERS[f][r] : FACE_CORNERS[f][r] + 1, :] for f in range(FACES)], axis=1
            )
            for part in (cvh, cvl)
            for r in range(4)
        ]
        * 2,
        axis=0,
    ).astype(BF16)
    ids = dot_nt(face_ids, shared)[:8]
    target = shared_target_row()
    for f in range(FACES):
        pl_ref[f * ELEMS : (f + 1) * ELEMS, :] = hot(columns[f] == target)
    for move in moves[3:]:
        move.wait()
    basis = bas_ref[...]
    stiff = stiff_of(jnp.concatenate([basis, basis], axis=0), bh_ref[...], bl_ref[...])
    lb_ref[:, :NODES] = tripled(basis)
    lb_ref[:, NODES:] = tripled(stiff[:8])
    kh, kl = split(inv_ref[...])
    kh_ref[...] = kh
    kl_ref[...] = kl

    state = tan_ref[...]
    advanced = advance(state, stiff_of(state, bh_ref[...], bl_ref[...]), met_ref[...], swl_ref[...])
    blocks, ah, al = face_blocks(advanced, sel_ref[...])
    pair_up(blocks, p_ref, q_ref, g_ref)
    out_ref[...] = settle(advanced, g_ref[...], sel_ref[...])
    coarse = coarse_of(ah, al, g_ref[...], bas_ref[...], pair_ref[...], cvh, bm_ref[...])
    y = dot(shared, q_ref[...])
    yh, yl = y[:, :HALO], y[:, HALO:]
    rf = two_products(pair_ref[...] * F32(0.5 / NODES), yh.astype(BF16), yl.astype(BF16))
    send_rows(msg_ref, me, jnp.concatenate([coarse, rf, ids], axis=0), yh + yl)


def second_kernel(
    s1_ref, got_ref, p_ref, bm_ref, bh_ref, bl_ref, kh_ref, kl_ref, pl_ref, lb_ref, swl_ref, met_ref, fs_ref, cor_ref,
    sel_ref, bas_ref, pair_ref,
    out_ref, msg_ref, q_ref, g_ref,
):
    me = lax.axis_index("dom")
    before, after = lax.rem(me + 7, 8), lax.rem(me + 1, 8)
    select = sel_ref[...]
    cvh, _ = corner_parts(cor_ref)
    cvh_row = row_of(cvh)
    which = iota((128, 1), 0).astype(F32)

    arrived = jnp.concatenate([got_ref[before, 24:MSG1, :], got_ref[after, 24:MSG1, :]], axis=0)
    partly = s1_ref[...] + F32(0.5) * halo_part(pl_ref[...], arrived, select)
    stiff = stiff_of(partly, bh_ref[...], bl_ref[...])

    coarse = got_ref[0, 0:8, :]
    for j in range(1, 8):
        coarse = coarse + got_ref[j, 0:8, :]
    rf = jnp.concatenate([got_ref[j, 8:16, :] for j in range(8)], axis=1)
    ids = jnp.concatenate([got_ref[j, 16:24, :] for j in range(8)], axis=1)
    from_left = jnp.concatenate([ids[:, 1024 - SHARED :], ids[:, : 1024 - SHARED]], axis=1)
    from_right = jnp.concatenate([ids[:, SHARED:], ids[:, :SHARED]], axis=1)
    partner = jnp.where((iota((1, 1024), 1) & SHARED) == 0, from_left, from_right)
    for r in range(4):
        low_hot = hot(partner[4 + r : 5 + r, :] == which)
        coarse = coarse + deposit(
            eight(rf[r : r + 1, :], rf[4 + r : 5 + r, :]), partner[r : r + 1, :], low_hot
        )
    solved = solve(coarse, kh_ref[...], kl_ref[...])
    both = dot_tn(corner_values(solved, cvh_row, bm_ref[...]), lb_ref[...])
    advanced = advance(partly - both[:, :NODES], stiff - both[:, NODES:], met_ref[...], swl_ref[...])
    blocks, ah, al = face_blocks(advanced, select)
    pair_up(blocks, p_ref, q_ref, g_ref)
    out_ref[...] = settle(advanced, g_ref[...], select)
    coarse = coarse_of(ah, al, g_ref[...], bas_ref[...], pair_ref[...], cvh, bm_ref[...])
    shared = hot(shared_target_column() == jnp.concatenate(slot_rows(fs_ref), axis=1))
    y = dot(shared, q_ref[...])
    yh, yl = y[:, :HALO], y[:, HALO:]
    rf = two_products(pair_ref[...] * F32(0.5 / NODES), yh.astype(BF16), yl.astype(BF16))
    mine = jnp.concatenate([got_ref[before, 16:24, SHARED:], got_ref[after, 16:24, :SHARED]], axis=1)
    for r in range(4):
        low_hot = hot(mine[4 + r : 5 + r, :] == which)
        coarse = coarse + deposit(eight(rf[r : r + 1, :], rf[4 + r : 5 + r, :]), mine[r : r + 1, :], low_hot)
    send_rows(msg_ref, me, coarse, yh + yl)


def pack_kernel(got_ref, kh_ref, kl_ref, out_ref):
    me = lax.axis_index("dom")
    coarse = got_ref[0, 0:8, :]
    for j in range(1, 8):
        coarse = coarse + got_ref[j, 0:8, :]
    out_ref[0:8, :] = solve(coarse, kh_ref[...], kl_ref[...])
    out_ref[8 : 8 + SHARED, :] = got_ref[lax.rem(me + 7, 8), 8:MSG2, :]
    out_ref[8 + SHARED :, :] = got_ref[lax.rem(me + 1, 8), 8:MSG2, :]


def last_kernel(tan_ref, s2_ref, small_ref, bm_ref, pl_ref, lb_ref, cor_ref, sel_ref, ang_ref, out_ref):
    cvh, _ = corner_parts(cor_ref)
    corners = corner_values(small_ref[0:8, :], row_of(cvh), bm_ref[...])
    state = (
        s2_ref[...]
        + F32(0.5) * halo_part(pl_ref[...], small_ref[8:, :], sel_ref[...])
        - dot_tn(corners, lb_ref[:, :NODES])
    )
    angle = jnp.where(lax.axis_index("seg") == 0, ang_ref[0], F32(0.0))
    angles = jnp.full((1, NODES), angle, F32)
    cosine, sine = jnp.cos(angles), jnp.sin(angles)
    re, im = state[:ELEMS], state[ELEMS:]
    out_ref[0:ELEMS, :] = tan_ref[0:ELEMS, :] - (cosine * re - sine * im)
    out_ref[ELEMS:, :] = tan_ref[ELEMS:, :] - (sine * re + cosine * im)


VMEM = pl.BlockSpec(memory_space=pltpu.VMEM)
SMEM = pl.BlockSpec(memory_space=pltpu.SMEM)
HBM = pl.BlockSpec(memory_space=pltpu.HBM)


def call(body, outs, scratch, ins, flops, specs=None, limit=28):
    size = sum(int(np.prod(o.shape)) * o.dtype.itemsize for o in outs)
    size += sum(int(np.prod(a.shape)) * a.dtype.itemsize for a in ins)
    return pl.pallas_call(
        body,
        out_shape=outs,
        in_specs=specs or [VMEM] * len(ins),
        out_specs=[VMEM] * len(outs),
        scratch_shapes=scratch,
        compiler_params=pltpu.CompilerParams(vmem_limit_bytes=limit * 1024 * 1024),
        cost_estimate=pl.CostEstimate(flops=flops, bytes_accessed=size, transcendentals=0),
    )(*ins)


def like(*shape, dtype=F32):
    return jax.ShapeDtypeStruct(shape, dtype)


def shards(tangent, base_swirl, metric, stiffness, face_slot, corners, coarse_inverse, phase_angle):
    basis, pair, select = tables()
    basis, pair, select = jnp.asarray(basis), jnp.asarray(pair), jnp.asarray(select, dtype=BF16)
    state = tangent.reshape(2 * ELEMS, NODES)
    swirl = base_swirl.reshape(ELEMS, NODES)
    slots = face_slot.T
    ids = corners.T
    field = like(2 * ELEMS, NODES)
    square = like(NODES, NODES, dtype=BF16)
    count = FACES * ELEMS
    faces = pltpu.VMEM((count, 2 * HALO), BF16)

    ins = [state, swirl, metric, stiffness, slots, ids, select, basis, pair, coarse_inverse]
    s1, msg, p, bm, bh, bl, kh, kl, placed, lb = call(
        first_kernel,
        [
            field,
            like(8, MSG1, 128),
            like(count, count, dtype=BF16),
            like(128, 8 * ELEMS, dtype=BF16),
            square,
            square,
            square,
            square,
            like(count, HALO, dtype=BF16),
            like(32, 2 * NODES, dtype=BF16),
        ],
        [faces, faces] + [pltpu.VMEM(a.shape, a.dtype) for a in ins] + [pltpu.SemaphoreType.DMA((len(ins),))],
        [pltpu.with_memory_space_constraint(a, pltpu.HBM) for a in ins],
        4_000_000_000,
        [HBM] * len(ins),
    )
    got = lax.all_to_all(msg, "dom", 0, 0)
    s2, msg = call(
        second_kernel,
        [field, like(8, MSG2, 128)],
        [faces, faces],
        [s1, got, p, bm, bh, bl, kh, kl, placed, lb, swirl, metric, slots, ids, select, basis, pair],
        4_000_000_000,
    )
    size = lax.axis_size("seg")
    ring = [(i, (i + 1) % size) for i in range(size)]
    got = lax.all_to_all(msg, "dom", 0, 0)
    s2 = lax.ppermute(s2, "seg", ring)
    (small,) = call(pack_kernel, [like(8 + HALO, 128)], [], [got, kh, kl], 100_000_000)
    small = lax.ppermute(small, "seg", ring)
    (out,) = call(
        last_kernel,
        [field],
        [],
        [state, s2, small, bm, placed, lb, ids, select, phase_angle],
        1_000_000_000,
        [VMEM] * 8 + [SMEM],
    )
    return out.reshape(1, 2, ELEMS, NODES)


def solution(mesh):
    return jax.shard_map(
        shards,
        mesh=mesh,
        in_specs=(
            P("seg", None, "dom", None),
            P("seg", "dom", None),
            P("dom", None),
            P(),
            P("dom", None),
            P("dom", None),
            P(),
            P(),
        ),
        out_specs=P("seg", None, "dom", None),
        check_vma=False,
    )
```

```python
import jax
import jax.numpy as jnp
import numpy as np
from jax import lax
from jax.experimental import pallas as pl
from jax.experimental.pallas import tpu as pltpu
from jax.sharding import PartitionSpec as P

F32 = jnp.float32
BF16 = jnp.bfloat16
NP = 8
NODES = 512
ELEMS = 256
FACES = 6
PLANE = 64
SHARED = 64
HALO = 2 * SHARED
INNER_TOP = 768
MSG1 = 88
FACE_CORNERS = (
    (0, 1, 2, 3),
    (4, 5, 6, 7),
    (0, 1, 4, 5),
    (2, 3, 6, 7),
    (0, 2, 4, 6),
    (1, 3, 5, 7),
)


def tables():
    points = -np.cos(np.pi * np.arange(NP) / (NP - 1))
    linear = np.stack([(1.0 - points) / 2.0, (1.0 + points) / 2.0])
    basis = (
        linear[:, None, None, :, None, None]
        * linear[None, :, None, None, :, None]
        * linear[None, None, :, None, None, :]
    ).reshape(8, NODES)
    flat = (linear[:, None, :, None] * linear[None, :, None, :]).reshape(4, PLANE)
    pair = np.zeros((8, 2 * PLANE))
    pair[:4, :PLANE] = flat
    pair[4:, PLANE:] = flat
    node = np.arange(NODES).reshape(NP, NP, NP)
    faces = [node[:, 0], node[:, -1], node[:, :, 0], node[:, :, -1]]
    chosen = np.concatenate([f.reshape(-1) for f in faces])
    select = (np.arange(NODES)[:, None] == chosen[None, :]).astype(np.float32)
    return basis.astype(np.float32), pair.astype(np.float32), select


def dot(a, b):
    return lax.dot_general(a, b, (((1,), (0,)), ((), ())), preferred_element_type=F32)


def dot_nt(a, b):
    return lax.dot_general(a, b, (((1,), (1,)), ((), ())), preferred_element_type=F32)


def dot_tn(a, b):
    return lax.dot_general(a, b, (((0,), (0,)), ((), ())), preferred_element_type=F32)


def split(x):
    high = x.astype(BF16)
    return high, (x - high.astype(F32)).astype(BF16)


def stacked(x):
    high = x.astype(BF16).astype(F32)
    return jnp.concatenate([high, x - high], axis=0).astype(BF16)


def hot(mask):
    return jnp.where(mask, F32(1.0), F32(0.0)).astype(BF16)


def iota(shape, dim):
    return lax.broadcasted_iota(jnp.int32, shape, dim)


def slot_rows(fs_ref):
    rows = fs_ref[...].astype(F32)
    return [rows[f : f + 1, :] for f in range(FACES)]


def slot_columns(fs_ref):
    rows = fs_ref[...].astype(F32)
    columns = jnp.concatenate([rows, rows[:2]], axis=0).T
    return [columns[:, f : f + 1] for f in range(FACES)]


def corner_parts(cor_ref):
    ids = cor_ref[...]
    return (ids >> 7).astype(F32), (ids & 127).astype(F32)


def row_of(parts):
    return jnp.concatenate([parts[k : k + 1, :] for k in range(parts.shape[0])], axis=1)


def stiff_of(state, bh, bl):
    high, low = split(state)
    return dot(high, bh) + dot(low, bh) + dot(high, bl)


def stiff_matrix(sti):
    rest = sti - sti.astype(BF16).astype(F32)
    low = rest - rest.astype(BF16).astype(F32)
    parts = jnp.concatenate(
        [sti.astype(BF16).astype(F32), rest.astype(BF16).astype(F32), low, jnp.zeros((8, 8), F32)], axis=0
    ).astype(BF16)
    row, col = iota((NODES, 8), 0), iota((NODES, 8), 1)
    col32, lane = iota((32, NODES), 0), iota((32, NODES), 1)
    from_n = iota((NODES, 1), 0)
    to_n = iota((1, NODES), 1)
    total = jnp.zeros((NODES, NODES), F32)
    for shift, keep in ((6, 63), (3, 455), (0, 504)):
        source = hot(((row >> shift) & 7) == col)
        target = hot(((lane >> shift) & 7) == (col32 & 7))
        spread = dot_nt(source, parts)
        spread = dot(spread.astype(BF16), target)
        same = (from_n & keep) == (to_n & keep)
        total = total + jnp.where(same, spread, F32(0.0))
    return total


def advance(state, stiff, metric, swirl):
    re, im = state[:ELEMS], state[ELEMS:]
    new_re = re - metric * stiff[:ELEMS] - swirl * im
    new_im = im - metric * stiff[ELEMS:] + swirl * re
    return jnp.concatenate([new_re, new_im], axis=0)


def face_blocks(advanced, select):
    ah, al = split(advanced)
    fh, fl = dot(ah, select), dot(al, select)
    high, low = ah.astype(F32), al.astype(F32)
    ends = (slice(0, PLANE), slice(NODES - PLANE, NODES))
    pairs = [(high[:, lanes], low[:, lanes]) for lanes in ends]
    for f in range(4):
        lanes = slice(f * PLANE, (f + 1) * PLANE)
        pairs.append((fh[:, lanes], fl[:, lanes]))
    blocks = [
        jnp.concatenate([h[:ELEMS], h[ELEMS:], l[:ELEMS], l[ELEMS:]], axis=1).astype(BF16) for h, l in pairs
    ]
    return blocks, ah, al


def scattered(blocks, select):
    def element_rows(faces, offset):
        re = jnp.concatenate([b[:, offset : offset + PLANE] for b in faces], axis=1)
        im = jnp.concatenate([b[:, offset + PLANE : offset + 2 * PLANE] for b in faces], axis=1)
        return jnp.concatenate([re, im], axis=0)

    high = element_rows(blocks[2:], 0).astype(BF16)
    low = element_rows(blocks[2:], HALO).astype(BF16)
    inner = dot_nt(high, select) + dot_nt(low, select)
    ends = []
    for block in blocks[:2]:
        both = block[:, :HALO] + block[:, HALO:]
        ends.append(jnp.concatenate([both[:, :PLANE], both[:, PLANE:]], axis=0))
    gap = jnp.zeros((2 * ELEMS, NODES - 2 * PLANE), F32)
    return inner + jnp.concatenate([ends[0], gap, ends[1]], axis=1)


def multiplicity():
    n = iota((1, NODES), 1)
    total = jnp.zeros((1, NODES), F32)
    for shift in (6, 3, 0):
        at = (n >> shift) & 7
        total = total + jnp.where((at == 0) | (at == 7), F32(1.0), F32(0.0))
    return total


def deposit(values, high_ids, low_hot):
    vh = (iota((8, 1), 0) & 3).astype(F32)
    chosen = jnp.where(high_ids == vh, values, F32(0.0))
    both = dot_nt(stacked(chosen), low_hot)
    return both[:8] + both[8:]


def eight(re, im):
    return jnp.where(iota((8, 1), 0) < 4, re, im)


def two_products(table, high, low):
    first = dot_nt(stacked(table), high)
    second = dot_nt(stacked(table), low)
    return first[:8] + first[8:] + second[:8]


def coarse_of(ah, al, partner, basis, pair, cvh, bm):
    own = two_products(basis * ((F32(1.0) - F32(0.5) * multiplicity()) * F32(1.0 / NODES)), ah, al)
    lifted = two_products(pair * F32(0.5 / NODES), partner[:, :HALO], partner[:, HALO:])
    values = []
    for k in range(8):
        total = eight(own[k : k + 1, :ELEMS], own[k : k + 1, ELEMS:])
        for f in range(FACES):
            if k in FACE_CORNERS[f]:
                r = FACE_CORNERS[f].index(k)
                lanes = slice(f * ELEMS, (f + 1) * ELEMS)
                total = total + eight(lifted[r : r + 1, lanes], lifted[4 + r : 5 + r, lanes])
        values.append(total)
    return deposit(jnp.concatenate(values, axis=1), row_of(cvh), bm)


def solve(coarse, kh, kl):
    rows = [jnp.concatenate([coarse[4 * c + h : 4 * c + h + 1] for h in range(4)], axis=1) for c in range(2)]
    flat = jnp.concatenate(rows, axis=0)
    high = flat.astype(BF16).astype(F32)
    packed = jnp.concatenate([high, flat - high, jnp.zeros((12, NODES), F32)], axis=0).astype(BF16)
    first = dot_nt(packed, kh)
    second = dot_nt(packed, kl)
    solved = first[0:2] + first[2:4] + second[0:2]
    return jnp.concatenate(
        [solved[c : c + 1, 128 * h : 128 * (h + 1)] for c in range(2) for h in range(4)], axis=0
    )


def corner_values(solved, cvh_row, bm):
    both = dot(stacked(solved), bm)
    spread = both[:8] + both[8:]
    vh = (iota((8, 1), 0) & 3).astype(F32)
    spread = jnp.where(cvh_row == vh, spread, F32(0.0))
    lines = []
    for c in range(2):
        line = jnp.sum(spread[4 * c : 4 * c + 4], axis=0, keepdims=True)
        lines.append(jnp.concatenate([line[:, ELEMS * k : ELEMS * (k + 1)] for k in range(8)], axis=0))
    by_corner = jnp.concatenate(lines, axis=1)
    high = by_corner.astype(BF16).astype(F32)
    return jnp.concatenate([high, by_corner - high, high, jnp.zeros((8, NODES), F32)], axis=0).astype(BF16)


def tripled(table):
    high = table.astype(BF16).astype(F32)
    return jnp.concatenate([high, high, table - high, jnp.zeros_like(high)], axis=0).astype(BF16)


def shared_target_column():
    s = iota((HALO, 1), 0)
    return jnp.where(s < SHARED, s, s + (INNER_TOP - SHARED)).astype(F32)


def shared_target_row():
    s = iota((1, HALO), 1)
    return jnp.where(s < SHARED, s, s + (INNER_TOP - SHARED)).astype(F32)


def halo_part(placed, arrived, select):
    high, low = split(arrived)
    both = jnp.concatenate([high.astype(F32), low.astype(F32)], axis=1).astype(BF16)
    got = dot(placed, both)
    return scattered([got[f * ELEMS : (f + 1) * ELEMS] for f in range(FACES)], select)


def settle(advanced, partner, select):
    blocks = [partner[f * ELEMS : (f + 1) * ELEMS].astype(F32) for f in range(FACES)]
    kept = advanced * (F32(1.0) - F32(0.5) * multiplicity())
    return kept + F32(0.5) * scattered(blocks, select)


def pair_up(blocks, p_ref, q_ref, g_ref):
    for f in range(FACES):
        q_ref[f * ELEMS : (f + 1) * ELEMS, :] = blocks[f]
    for f in range(FACES):
        rows = slice(f * ELEMS, (f + 1) * ELEMS)
        g_ref[rows, :] = dot(p_ref[rows, :], q_ref[...]).astype(BF16)


def send_rows(msg_ref, me, head, rows):
    count = head.shape[0]
    up, down = rows[:SHARED], rows[SHARED:]
    after = lax.rem(me + 1, 8)
    for j in range(8):
        msg_ref[j, 0:count, :] = head
        msg_ref[j, count : count + SHARED, :] = jnp.where(after == j, down, up)


def first_kernel(
    tan_hbm, swl_hbm, met_hbm, sti_hbm, fs_hbm, cor_hbm, sel_hbm, bas_hbm, pair_hbm, inv_hbm,
    out_ref, msg_ref, p_ref, bm_ref, bh_ref, bl_ref, kh_ref, kl_ref, pl_ref, lb_ref,
    q_ref, g_ref, tan_ref, swl_ref, met_ref, sti_ref, fs_ref, cor_ref, sel_ref, bas_ref, pair_ref, inv_ref, sems,
):
    me = lax.axis_index("dom")
    moves = [
        pltpu.make_async_copy(src, dst, sems.at[i])
        for i, (src, dst) in enumerate(
            (
                (sti_hbm, sti_ref),
                (fs_hbm, fs_ref),
                (cor_hbm, cor_ref),
                (tan_hbm, tan_ref),
                (met_hbm, met_ref),
                (swl_hbm, swl_ref),
                (sel_hbm, sel_ref),
                (bas_hbm, bas_ref),
                (pair_hbm, pair_ref),
                (inv_hbm, inv_ref),
            )
        )
    ]
    for move in moves:
        move.start()
    for move in moves[:3]:
        move.wait()
    bh, bl = split(stiff_matrix(sti_ref[...]))
    bh_ref[...] = bh
    bl_ref[...] = bl
    rows = slot_rows(fs_ref)
    columns = slot_columns(fs_ref)
    other = iota((ELEMS, 1), 0) != iota((1, ELEMS), 1)
    for f in range(FACES):
        for g in range(FACES):
            same = columns[f] == rows[g]
            if f == g:
                same = same & other
            p_ref[f * ELEMS : (f + 1) * ELEMS, g * ELEMS : (g + 1) * ELEMS] = hot(same)
    cvh, cvl = corner_parts(cor_ref)
    bm_ref[...] = hot(row_of(cvl) == iota((128, 1), 0).astype(F32))
    shared = hot(shared_target_column() == jnp.concatenate(rows, axis=1))
    face_ids = jnp.concatenate(
        [
            jnp.concatenate(
                [part[FACE_CORNERS[f][r] : FACE_CORNERS[f][r] + 1, :] for f in range(FACES)], axis=1
            )
            for part in (cvh, cvl)
            for r in range(4)
        ]
        * 2,
        axis=0,
    ).astype(BF16)
    ids = dot_nt(face_ids, shared)[:8]
    target = shared_target_row()
    for f in range(FACES):
        pl_ref[f * ELEMS : (f + 1) * ELEMS, :] = hot(columns[f] == target)
    for move in moves[3:]:
        move.wait()
    basis = bas_ref[...]
    stiff = stiff_of(jnp.concatenate([basis, basis], axis=0), bh_ref[...], bl_ref[...])
    lb_ref[:, :NODES] = tripled(basis)
    lb_ref[:, NODES:] = tripled(stiff[:8])
    kh, kl = split(inv_ref[...])
    kh_ref[...] = kh
    kl_ref[...] = kl

    state = tan_ref[...]
    advanced = advance(state, stiff_of(state, bh_ref[...], bl_ref[...]), met_ref[...], swl_ref[...])
    blocks, ah, al = face_blocks(advanced, sel_ref[...])
    pair_up(blocks, p_ref, q_ref, g_ref)
    out_ref[...] = settle(advanced, g_ref[...], sel_ref[...])
    coarse = coarse_of(ah, al, g_ref[...], bas_ref[...], pair_ref[...], cvh, bm_ref[...])
    y = dot(shared, q_ref[...])
    yh, yl = y[:, :HALO], y[:, HALO:]
    rf = two_products(pair_ref[...] * F32(0.5 / NODES), yh.astype(BF16), yl.astype(BF16))
    send_rows(msg_ref, me, jnp.concatenate([coarse, rf, ids], axis=0), yh + yl)


def second_kernel(
    s1_ref, got_ref, p_ref, bm_ref, bh_ref, bl_ref, kh_ref, kl_ref, pl_ref, lb_ref, swl_ref, met_ref, fs_ref, cor_ref,
    sel_ref, bas_ref, pair_ref,
    out_ref, msg_ref, near_ref, q_ref, g_ref,
):
    me = lax.axis_index("dom")
    before, after = lax.rem(me + 7, 8), lax.rem(me + 1, 8)
    select = sel_ref[...]
    cvh, _ = corner_parts(cor_ref)
    cvh_row = row_of(cvh)
    which = iota((128, 1), 0).astype(F32)

    arrived = jnp.concatenate([got_ref[before, 24:MSG1, :], got_ref[after, 24:MSG1, :]], axis=0)
    partly = s1_ref[...] + F32(0.5) * halo_part(pl_ref[...], arrived, select)
    stiff = stiff_of(partly, bh_ref[...], bl_ref[...])

    coarse = got_ref[0, 0:8, :]
    for j in range(1, 8):
        coarse = coarse + got_ref[j, 0:8, :]
    rf = jnp.concatenate([got_ref[j, 8:16, :] for j in range(8)], axis=1)
    ids = jnp.concatenate([got_ref[j, 16:24, :] for j in range(8)], axis=1)
    from_left = jnp.concatenate([ids[:, 1024 - SHARED :], ids[:, : 1024 - SHARED]], axis=1)
    from_right = jnp.concatenate([ids[:, SHARED:], ids[:, :SHARED]], axis=1)
    partner = jnp.where((iota((1, 1024), 1) & SHARED) == 0, from_left, from_right)
    for r in range(4):
        low_hot = hot(partner[4 + r : 5 + r, :] == which)
        coarse = coarse + deposit(
            eight(rf[r : r + 1, :], rf[4 + r : 5 + r, :]), partner[r : r + 1, :], low_hot
        )
    solved = solve(coarse, kh_ref[...], kl_ref[...])
    both = dot_tn(corner_values(solved, cvh_row, bm_ref[...]), lb_ref[...])
    advanced = advance(partly - both[:, :NODES], stiff - both[:, NODES:], met_ref[...], swl_ref[...])
    blocks, ah, al = face_blocks(advanced, select)
    pair_up(blocks, p_ref, q_ref, g_ref)
    out_ref[...] = settle(advanced, g_ref[...], select)
    coarse = coarse_of(ah, al, g_ref[...], bas_ref[...], pair_ref[...], cvh, bm_ref[...])
    shared = hot(shared_target_column() == jnp.concatenate(slot_rows(fs_ref), axis=1))
    y = dot(shared, q_ref[...])
    yh, yl = y[:, :HALO], y[:, HALO:]
    rf = two_products(pair_ref[...] * F32(0.5 / NODES), yh.astype(BF16), yl.astype(BF16))
    mine = jnp.concatenate([got_ref[before, 16:24, SHARED:], got_ref[after, 16:24, :SHARED]], axis=1)
    for r in range(4):
        low_hot = hot(mine[4 + r : 5 + r, :] == which)
        coarse = coarse + deposit(eight(rf[r : r + 1, :], rf[4 + r : 5 + r, :]), mine[r : r + 1, :], low_hot)
    rows = yh + yl
    even = (me & 1) == 0
    near_ref[...] = jnp.where(even, rows[SHARED:], rows[:SHARED])
    far = jnp.where(even, rows[:SHARED], rows[SHARED:])
    for j in range(4):
        msg_ref[j, 0:8, :] = coarse
        msg_ref[j, 8:, :] = far


def pack_kernel(got_ref, near_ref, sum_ref, across_ref):
    me = lax.axis_index("dom")
    coarse = got_ref[0, 0:8, :]
    for j in range(1, 4):
        coarse = coarse + got_ref[j, 0:8, :]
    sum_ref[...] = coarse
    across_ref[0:8, :] = coarse
    across_ref[8 : 8 + SHARED, :] = near_ref[...]
    giver = (me // 2 + jnp.where((me & 1) == 0, 1, 3)) & 3
    across_ref[8 + SHARED :, :] = got_ref[giver, 8:, :]


def prepare_kernel(lb_ref, cor_ref, fs_ref, ang_ref, bm_ref, bas_ref, pl_ref, sel_ref, turn_ref):
    angle = jnp.where(lax.axis_index("seg") == 0, ang_ref[0], F32(0.0))
    angles = jnp.full((8, 128), angle, F32)
    turn_ref[0:8, :] = jnp.cos(angles)
    turn_ref[8:16, :] = jnp.sin(angles)
    _, cvl = corner_parts(cor_ref)
    bm_ref[...] = hot(row_of(cvl) == iota((128, 1), 0).astype(F32))
    bas_ref[...] = lb_ref[:, :NODES]
    columns = slot_columns(fs_ref)
    target = shared_target_row()
    for f in range(FACES):
        pl_ref[f * ELEMS : (f + 1) * ELEMS, :] = hot(columns[f] == target)
    lane = iota((1, 4 * PLANE), 1)
    face, p, q = lane >> 6, (lane >> 3) & 7, lane & 7
    middle = p * PLANE + q + jnp.where(face == 1, 56, 0)
    outer = p * PLANE + q * 8 + jnp.where(face == 3, 7, 0)
    sel_ref[...] = hot(iota((NODES, 1), 0) == jnp.where(face < 2, middle, outer))


def last_kernel(
    tan_ref, s2_ref, sum_ref, across_ref, kh_ref, kl_ref, bm_ref, bas_ref, pl_ref, sel_ref, cor_ref, turn_ref,
    out_ref,
):
    even = (lax.axis_index("dom") & 1) == 0
    near, far = across_ref[8 : 8 + SHARED, :], across_ref[8 + SHARED :, :]
    arrived = jnp.concatenate([jnp.where(even, far, near), jnp.where(even, near, far)], axis=0)
    partly = s2_ref[...] + F32(0.5) * halo_part(pl_ref[...], arrived, sel_ref[...])
    cvh, _ = corner_parts(cor_ref)
    solved = solve(sum_ref[...] + across_ref[0:8, :], kh_ref[...], kl_ref[...])
    state = partly - dot_tn(corner_values(solved, row_of(cvh), bm_ref[...]), bas_ref[...])
    cosine = jnp.concatenate([turn_ref[0:1, :]] * 4, axis=1)
    sine = jnp.concatenate([turn_ref[8:9, :]] * 4, axis=1)
    re, im = state[:ELEMS], state[ELEMS:]
    out_ref[0:ELEMS, :] = tan_ref[0:ELEMS, :] - (cosine * re - sine * im)
    out_ref[ELEMS:, :] = tan_ref[ELEMS:, :] - (sine * re + cosine * im)


VMEM = pl.BlockSpec(memory_space=pltpu.VMEM)
HBM = pl.BlockSpec(memory_space=pltpu.HBM)


def call(body, outs, scratch, ins, flops, specs=None, outs_at=None, limit=28):
    size = sum(int(np.prod(o.shape)) * o.dtype.itemsize for o in outs)
    size += sum(int(np.prod(a.shape)) * a.dtype.itemsize for a in ins)
    return pl.pallas_call(
        body,
        out_shape=outs,
        in_specs=specs or [VMEM] * len(ins),
        out_specs=outs_at or [VMEM] * len(outs),
        scratch_shapes=scratch,
        compiler_params=pltpu.CompilerParams(vmem_limit_bytes=limit * 1024 * 1024),
        cost_estimate=pl.CostEstimate(flops=flops, bytes_accessed=size, transcendentals=0),
    )(*ins)


def like(*shape, dtype=F32):
    return jax.ShapeDtypeStruct(shape, dtype)


def shards(tangent, base_swirl, metric, stiffness, face_slot, corners, coarse_inverse, phase_angle):
    basis, pair, select = tables()
    basis, pair, select = jnp.asarray(basis), jnp.asarray(pair), jnp.asarray(select, dtype=BF16)
    state = tangent.reshape(2 * ELEMS, NODES)
    swirl = base_swirl.reshape(ELEMS, NODES)
    slots = face_slot.T
    ids = corners.T
    field = like(2 * ELEMS, NODES)
    square = like(NODES, NODES, dtype=BF16)
    count = FACES * ELEMS
    faces = pltpu.VMEM((count, 2 * HALO), BF16)

    ins = [state, swirl, metric, stiffness, slots, ids, select, basis, pair, coarse_inverse]
    s1, msg, p, bm, bh, bl, kh, kl, placed, lb = call(
        first_kernel,
        [
            field,
            like(8, MSG1, 128),
            like(count, count, dtype=BF16),
            like(128, 8 * ELEMS, dtype=BF16),
            square,
            square,
            square,
            square,
            like(count, HALO, dtype=BF16),
            like(32, 2 * NODES, dtype=BF16),
        ],
        [faces, faces]
        + [pltpu.VMEM(a.shape, a.dtype) for a in ins]
        + [pltpu.SemaphoreType.DMA((len(ins),))],
        [pltpu.with_memory_space_constraint(a, pltpu.HBM) for a in ins],
        4_000_000_000,
        [HBM] * len(ins),
    )
    got = lax.all_to_all(msg, "dom", 0, 0)
    s2, msg, near = call(
        second_kernel,
        [field, like(4, 8 + SHARED, 128), like(SHARED, 128)],
        [faces, faces],
        [s1, got, p, bm, bh, bl, kh, kl, placed, lb, swirl, metric, slots, ids, select, basis, pair],
        4_000_000_000,
    )
    size = lax.axis_size("seg")
    ring = [(i, (i + 1) % size) for i in range(size)]

    def onward(target):
        return [(8 * i + d, 8 * j + target(d)) for i, j in ring for d in range(8)]

    s2 = lax.ppermute(s2, "seg", ring)
    got = lax.all_to_all(msg, "dom", 0, 0, axis_index_groups=[[0, 2, 4, 6], [1, 3, 5, 7]])
    total, across = call(pack_kernel, [like(8, 128), like(8 + HALO, 128)], [], [got, near], 1_000_000)
    across = lax.ppermute(across, ("seg", "dom"), onward(lambda d: d ^ 1))
    total = lax.ppermute(total, "seg", ring)
    bm, wide, placed, select, turn = call(
        prepare_kernel,
        [
            like(128, 8 * ELEMS, dtype=BF16),
            like(32, NODES, dtype=BF16),
            like(count, HALO, dtype=BF16),
            like(NODES, 4 * PLANE, dtype=BF16),
            like(16, 128),
        ],
        [],
        [lb, ids, slots, phase_angle],
        1_000_000_000,
        [VMEM] * 3 + [pl.BlockSpec(memory_space=pltpu.SMEM)],
    )
    (out,) = call(
        last_kernel,
        [field],
        [],
        [state, s2, total, across, kh, kl, bm, wide, placed, select, ids, turn],
        1_000_000_000,
    )
    return out.reshape(1, 2, ELEMS, NODES)


def solution(mesh):
    return jax.shard_map(
        shards,
        mesh=mesh,
        in_specs=(
            P("seg", None, "dom", None),
            P("seg", "dom", None),
            P("dom", None),
            P(),
            P("dom", None),
            P("dom", None),
            P(),
            P(),
        ),
        out_specs=P("seg", None, "dom", None),
        check_vma=False,
    )
```

```python
import jax
import jax.numpy as jnp
import numpy as np
from jax import lax
from jax.experimental import pallas as pl
from jax.experimental.pallas import tpu as pltpu
from jax.sharding import PartitionSpec as P

F32 = jnp.float32
BF16 = jnp.bfloat16
NP = 8
NODES = 512
ELEMS = 256
FACES = 6
PLANE = 64
SHARED = 64
HALO = 2 * SHARED
INNER_TOP = 768
MSG1 = 88
FACE_CORNERS = (
    (0, 1, 2, 3),
    (4, 5, 6, 7),
    (0, 1, 4, 5),
    (2, 3, 6, 7),
    (0, 2, 4, 6),
    (1, 3, 5, 7),
)


def tables():
    points = -np.cos(np.pi * np.arange(NP) / (NP - 1))
    linear = np.stack([(1.0 - points) / 2.0, (1.0 + points) / 2.0])
    basis = (
        linear[:, None, None, :, None, None]
        * linear[None, :, None, None, :, None]
        * linear[None, None, :, None, None, :]
    ).reshape(8, NODES)
    flat = (linear[:, None, :, None] * linear[None, :, None, :]).reshape(4, PLANE)
    pair = np.zeros((8, 2 * PLANE))
    pair[:4, :PLANE] = flat
    pair[4:, PLANE:] = flat
    node = np.arange(NODES).reshape(NP, NP, NP)
    faces = [node[:, 0], node[:, -1], node[:, :, 0], node[:, :, -1]]
    chosen = np.concatenate([f.reshape(-1) for f in faces])
    select = (np.arange(NODES)[:, None] == chosen[None, :]).astype(np.float32)
    return basis.astype(np.float32), pair.astype(np.float32), select


def dot(a, b):
    return lax.dot_general(a, b, (((1,), (0,)), ((), ())), preferred_element_type=F32)


def dot_nt(a, b):
    return lax.dot_general(a, b, (((1,), (1,)), ((), ())), preferred_element_type=F32)


def dot_tn(a, b):
    return lax.dot_general(a, b, (((0,), (0,)), ((), ())), preferred_element_type=F32)


def split(x):
    high = x.astype(BF16)
    return high, (x - high.astype(F32)).astype(BF16)


def stacked(x):
    high = x.astype(BF16).astype(F32)
    return jnp.concatenate([high, x - high], axis=0).astype(BF16)


def hot(mask):
    return jnp.where(mask, F32(1.0), F32(0.0)).astype(BF16)


def iota(shape, dim):
    return lax.broadcasted_iota(jnp.int32, shape, dim)


def slot_rows(fs_ref):
    rows = fs_ref[...].astype(F32)
    return [rows[f : f + 1, :] for f in range(FACES)]


def slot_columns(fs_ref):
    rows = fs_ref[...].astype(F32)
    columns = jnp.concatenate([rows, rows[:2]], axis=0).T
    return [columns[:, f : f + 1] for f in range(FACES)]


def corner_parts(cor_ref):
    ids = cor_ref[...]
    return (ids >> 7).astype(F32), (ids & 127).astype(F32)


def row_of(parts):
    return jnp.concatenate([parts[k : k + 1, :] for k in range(parts.shape[0])], axis=1)


def stiff_of(state, bh, bl):
    high, low = split(state)
    return dot(high, bh) + dot(low, bh) + dot(high, bl)


def stiff_matrix(sti):
    rest = sti - sti.astype(BF16).astype(F32)
    low = rest - rest.astype(BF16).astype(F32)
    parts = jnp.concatenate(
        [sti.astype(BF16).astype(F32), rest.astype(BF16).astype(F32), low, jnp.zeros((8, 8), F32)], axis=0
    ).astype(BF16)
    row, col = iota((NODES, 8), 0), iota((NODES, 8), 1)
    col32, lane = iota((32, NODES), 0), iota((32, NODES), 1)
    from_n = iota((NODES, 1), 0)
    to_n = iota((1, NODES), 1)
    total = jnp.zeros((NODES, NODES), F32)
    for shift, keep in ((6, 63), (3, 455), (0, 504)):
        source = hot(((row >> shift) & 7) == col)
        target = hot(((lane >> shift) & 7) == (col32 & 7))
        spread = dot_nt(source, parts)
        spread = dot(spread.astype(BF16), target)
        same = (from_n & keep) == (to_n & keep)
        total = total + jnp.where(same, spread, F32(0.0))
    return total


def advance(state, stiff, metric, swirl):
    re, im = state[:ELEMS], state[ELEMS:]
    new_re = re - metric * stiff[:ELEMS] - swirl * im
    new_im = im - metric * stiff[ELEMS:] + swirl * re
    return jnp.concatenate([new_re, new_im], axis=0)


def face_blocks(advanced, select):
    ah, al = split(advanced)
    fh, fl = dot(ah, select), dot(al, select)
    high, low = ah.astype(F32), al.astype(F32)
    ends = (slice(0, PLANE), slice(NODES - PLANE, NODES))
    pairs = [(high[:, lanes], low[:, lanes]) for lanes in ends]
    for f in range(4):
        lanes = slice(f * PLANE, (f + 1) * PLANE)
        pairs.append((fh[:, lanes], fl[:, lanes]))
    blocks = [
        jnp.concatenate([h[:ELEMS], h[ELEMS:], l[:ELEMS], l[ELEMS:]], axis=1).astype(BF16) for h, l in pairs
    ]
    return blocks, ah, al


def scattered(blocks, select):
    def element_rows(faces, offset):
        re = jnp.concatenate([b[:, offset : offset + PLANE] for b in faces], axis=1)
        im = jnp.concatenate([b[:, offset + PLANE : offset + 2 * PLANE] for b in faces], axis=1)
        return jnp.concatenate([re, im], axis=0)

    high = element_rows(blocks[2:], 0).astype(BF16)
    low = element_rows(blocks[2:], HALO).astype(BF16)
    inner = dot_nt(high, select) + dot_nt(low, select)
    ends = []
    for block in blocks[:2]:
        both = block[:, :HALO] + block[:, HALO:]
        ends.append(jnp.concatenate([both[:, :PLANE], both[:, PLANE:]], axis=0))
    gap = jnp.zeros((2 * ELEMS, NODES - 2 * PLANE), F32)
    return inner + jnp.concatenate([ends[0], gap, ends[1]], axis=1)


def multiplicity():
    n = iota((1, NODES), 1)
    total = jnp.zeros((1, NODES), F32)
    for shift in (6, 3, 0):
        at = (n >> shift) & 7
        total = total + jnp.where((at == 0) | (at == 7), F32(1.0), F32(0.0))
    return total


def deposit(values, high_ids, low_hot):
    vh = (iota((8, 1), 0) & 3).astype(F32)
    chosen = jnp.where(high_ids == vh, values, F32(0.0))
    both = dot_nt(stacked(chosen), low_hot)
    return both[:8] + both[8:]


def eight(re, im):
    return jnp.where(iota((8, 1), 0) < 4, re, im)


def two_products(table, high, low):
    first = dot_nt(stacked(table), high)
    second = dot_nt(stacked(table), low)
    return first[:8] + first[8:] + second[:8]


def coarse_of(ah, al, partner, basis, pair, cvh, bm):
    own = two_products(basis * ((F32(1.0) - F32(0.5) * multiplicity()) * F32(1.0 / NODES)), ah, al)
    lifted = two_products(pair * F32(0.5 / NODES), partner[:, :HALO], partner[:, HALO:])
    values = []
    for k in range(8):
        total = eight(own[k : k + 1, :ELEMS], own[k : k + 1, ELEMS:])
        for f in range(FACES):
            if k in FACE_CORNERS[f]:
                r = FACE_CORNERS[f].index(k)
                lanes = slice(f * ELEMS, (f + 1) * ELEMS)
                total = total + eight(lifted[r : r + 1, lanes], lifted[4 + r : 5 + r, lanes])
        values.append(total)
    return deposit(jnp.concatenate(values, axis=1), row_of(cvh), bm)


def solve(coarse, kh, kl):
    rows = [jnp.concatenate([coarse[4 * c + h : 4 * c + h + 1] for h in range(4)], axis=1) for c in range(2)]
    flat = jnp.concatenate(rows, axis=0)
    high = flat.astype(BF16).astype(F32)
    packed = jnp.concatenate([high, flat - high, jnp.zeros((12, NODES), F32)], axis=0).astype(BF16)
    first = dot_nt(packed, kh)
    second = dot_nt(packed, kl)
    solved = first[0:2] + first[2:4] + second[0:2]
    return jnp.concatenate(
        [solved[c : c + 1, 128 * h : 128 * (h + 1)] for c in range(2) for h in range(4)], axis=0
    )


def corner_values(solved, cvh_row, bm):
    both = dot(stacked(solved), bm)
    spread = both[:8] + both[8:]
    vh = (iota((8, 1), 0) & 3).astype(F32)
    spread = jnp.where(cvh_row == vh, spread, F32(0.0))
    lines = []
    for c in range(2):
        line = jnp.sum(spread[4 * c : 4 * c + 4], axis=0, keepdims=True)
        lines.append(jnp.concatenate([line[:, ELEMS * k : ELEMS * (k + 1)] for k in range(8)], axis=0))
    by_corner = jnp.concatenate(lines, axis=1)
    high = by_corner.astype(BF16).astype(F32)
    return jnp.concatenate([high, by_corner - high, high, jnp.zeros((8, NODES), F32)], axis=0).astype(BF16)


def tripled(table):
    high = table.astype(BF16).astype(F32)
    return jnp.concatenate([high, high, table - high, jnp.zeros_like(high)], axis=0).astype(BF16)


def shared_target_column():
    s = iota((HALO, 1), 0)
    return jnp.where(s < SHARED, s, s + (INNER_TOP - SHARED)).astype(F32)


def shared_target_row():
    s = iota((1, HALO), 1)
    return jnp.where(s < SHARED, s, s + (INNER_TOP - SHARED)).astype(F32)


def halo_faces(placed, arrived):
    high, low = split(arrived)
    both = jnp.concatenate([high.astype(F32), low.astype(F32)], axis=1).astype(BF16)
    return dot(placed, both)


def halo_part(placed, arrived, select):
    got = halo_faces(placed, arrived)
    return scattered([got[f * ELEMS : (f + 1) * ELEMS] for f in range(FACES)], select)


def settle(advanced, partner, select):
    blocks = [partner[f * ELEMS : (f + 1) * ELEMS] for f in range(FACES)]
    kept = advanced * (F32(1.0) - F32(0.5) * multiplicity())
    return kept + F32(0.5) * scattered(blocks, select)


def pair_up(blocks, p_ref, q_ref, g_ref):
    for f in range(FACES):
        q_ref[f * ELEMS : (f + 1) * ELEMS, :] = blocks[f]
    for f in range(FACES):
        rows = slice(f * ELEMS, (f + 1) * ELEMS)
        g_ref[rows, :] = dot(p_ref[rows, :], q_ref[...]).astype(BF16)


def send_rows(msg_ref, me, head, rows):
    count = head.shape[0]
    up, down = rows[:SHARED], rows[SHARED:]
    after = lax.rem(me + 1, 8)
    for j in range(8):
        msg_ref[j, 0:count, :] = head
        msg_ref[j, count : count + SHARED, :] = jnp.where(after == j, down, up)


def first_kernel(
    tan_hbm, swl_hbm, met_hbm, sti_hbm, fs_hbm, cor_hbm, sel_hbm, bas_hbm, pair_hbm, inv_hbm,
    adv_ref, g_ref, msg_ref, p_ref, bm_ref, bh_ref, bl_ref, kh_ref, kl_ref, pl_ref, lb_ref,
    q_ref, tan_ref, swl_ref, met_ref, sti_ref, fs_ref, cor_ref, sel_ref, bas_ref, pair_ref, inv_ref, sems,
):
    me = lax.axis_index("dom")
    moves = [
        pltpu.make_async_copy(src, dst, sems.at[i])
        for i, (src, dst) in enumerate(
            (
                (sti_hbm, sti_ref),
                (fs_hbm, fs_ref),
                (cor_hbm, cor_ref),
                (tan_hbm, tan_ref),
                (met_hbm, met_ref),
                (swl_hbm, swl_ref),
                (sel_hbm, sel_ref),
                (bas_hbm, bas_ref),
                (pair_hbm, pair_ref),
                (inv_hbm, inv_ref),
            )
        )
    ]
    for move in moves:
        move.start()
    for move in moves[:3]:
        move.wait()
    bh, bl = split(stiff_matrix(sti_ref[...]))
    bh_ref[...] = bh
    bl_ref[...] = bl
    rows = slot_rows(fs_ref)
    columns = slot_columns(fs_ref)
    other = iota((ELEMS, 1), 0) != iota((1, ELEMS), 1)
    for f in range(FACES):
        for g in range(FACES):
            same = columns[f] == rows[g]
            if f == g:
                same = same & other
            p_ref[f * ELEMS : (f + 1) * ELEMS, g * ELEMS : (g + 1) * ELEMS] = hot(same)
    cvh, cvl = corner_parts(cor_ref)
    bm_ref[...] = hot(row_of(cvl) == iota((128, 1), 0).astype(F32))
    shared = hot(shared_target_column() == jnp.concatenate(rows, axis=1))
    face_ids = jnp.concatenate(
        [
            jnp.concatenate(
                [part[FACE_CORNERS[f][r] : FACE_CORNERS[f][r] + 1, :] for f in range(FACES)], axis=1
            )
            for part in (cvh, cvl)
            for r in range(4)
        ]
        * 2,
        axis=0,
    ).astype(BF16)
    ids = dot_nt(face_ids, shared)[:8]
    target = shared_target_row()
    for f in range(FACES):
        pl_ref[f * ELEMS : (f + 1) * ELEMS, :] = hot(columns[f] == target)
    for move in moves[3:9]:
        move.wait()
    basis = bas_ref[...]
    stiff = stiff_of(jnp.concatenate([basis, basis], axis=0), bh_ref[...], bl_ref[...])
    lb_ref[:, :NODES] = tripled(basis)
    lb_ref[:, NODES:] = tripled(stiff[:8])

    state = tan_ref[...]
    advanced = advance(state, stiff_of(state, bh_ref[...], bl_ref[...]), met_ref[...], swl_ref[...])
    adv_ref[...] = advanced
    blocks, ah, al = face_blocks(advanced, sel_ref[...])
    pair_up(blocks, p_ref, q_ref, g_ref)
    coarse = coarse_of(ah, al, g_ref[...], bas_ref[...], pair_ref[...], cvh, bm_ref[...])
    y = dot(shared, q_ref[...])
    yh, yl = y[:, :HALO], y[:, HALO:]
    rf = two_products(pair_ref[...] * F32(0.5 / NODES), yh.astype(BF16), yl.astype(BF16))
    send_rows(msg_ref, me, jnp.concatenate([coarse, rf, ids], axis=0), yh + yl)
    moves[9].wait()
    kh, kl = split(inv_ref[...])
    kh_ref[...] = kh
    kl_ref[...] = kl


def second_kernel(
    adv_ref, g1_ref, got_ref, p_ref, bm_ref, bh_ref, bl_ref, kh_ref, kl_ref, pl_ref, lb_ref, swl_ref, met_ref, fs_ref, cor_ref,
    sel_ref, bas_ref, pair_ref,
    out_ref, msg_ref, near_ref, q_ref, g_ref,
):
    me = lax.axis_index("dom")
    before, after = lax.rem(me + 7, 8), lax.rem(me + 1, 8)
    select = sel_ref[...]
    cvh, _ = corner_parts(cor_ref)
    cvh_row = row_of(cvh)
    which = iota((128, 1), 0).astype(F32)

    arrived = jnp.concatenate([got_ref[before, 24:MSG1, :], got_ref[after, 24:MSG1, :]], axis=0)
    partner = g1_ref[...].astype(F32) + halo_faces(pl_ref[...], arrived)
    partly = settle(adv_ref[...], partner, select)
    stiff = stiff_of(partly, bh_ref[...], bl_ref[...])

    coarse = got_ref[0, 0:8, :]
    for j in range(1, 8):
        coarse = coarse + got_ref[j, 0:8, :]
    rf = jnp.concatenate([got_ref[j, 8:16, :] for j in range(8)], axis=1)
    ids = jnp.concatenate([got_ref[j, 16:24, :] for j in range(8)], axis=1)
    from_left = jnp.concatenate([ids[:, 1024 - SHARED :], ids[:, : 1024 - SHARED]], axis=1)
    from_right = jnp.concatenate([ids[:, SHARED:], ids[:, :SHARED]], axis=1)
    partner = jnp.where((iota((1, 1024), 1) & SHARED) == 0, from_left, from_right)
    for r in range(4):
        low_hot = hot(partner[4 + r : 5 + r, :] == which)
        coarse = coarse + deposit(
            eight(rf[r : r + 1, :], rf[4 + r : 5 + r, :]), partner[r : r + 1, :], low_hot
        )
    solved = solve(coarse, kh_ref[...], kl_ref[...])
    both = dot_tn(corner_values(solved, cvh_row, bm_ref[...]), lb_ref[...])
    advanced = advance(partly - both[:, :NODES], stiff - both[:, NODES:], met_ref[...], swl_ref[...])
    blocks, ah, al = face_blocks(advanced, select)
    pair_up(blocks, p_ref, q_ref, g_ref)
    out_ref[...] = settle(advanced, g_ref[...].astype(F32), select)
    coarse = coarse_of(ah, al, g_ref[...], bas_ref[...], pair_ref[...], cvh, bm_ref[...])
    shared = hot(shared_target_column() == jnp.concatenate(slot_rows(fs_ref), axis=1))
    y = dot(shared, q_ref[...])
    yh, yl = y[:, :HALO], y[:, HALO:]
    rf = two_products(pair_ref[...] * F32(0.5 / NODES), yh.astype(BF16), yl.astype(BF16))
    mine = jnp.concatenate([got_ref[before, 16:24, SHARED:], got_ref[after, 16:24, :SHARED]], axis=1)
    for r in range(4):
        low_hot = hot(mine[4 + r : 5 + r, :] == which)
        coarse = coarse + deposit(eight(rf[r : r + 1, :], rf[4 + r : 5 + r, :]), mine[r : r + 1, :], low_hot)
    rows = yh + yl
    even = (me & 1) == 0
    near_ref[...] = jnp.where(even, rows[SHARED:], rows[:SHARED])
    far = jnp.where(even, rows[:SHARED], rows[SHARED:])
    for j in range(4):
        msg_ref[j, 0:8, :] = coarse
        msg_ref[j, 8:, :] = far


def pack_kernel(got_ref, near_ref, sum_ref, across_ref):
    me = lax.axis_index("dom")
    coarse = got_ref[0, 0:8, :]
    for j in range(1, 4):
        coarse = coarse + got_ref[j, 0:8, :]
    sum_ref[...] = coarse
    across_ref[0:8, :] = coarse
    across_ref[8 : 8 + SHARED, :] = near_ref[...]
    giver = (me // 2 + jnp.where((me & 1) == 0, 1, 3)) & 3
    across_ref[8 + SHARED :, :] = got_ref[giver, 8:, :]


def prepare_kernel(lb_ref, cor_ref, fs_ref, ang_ref, bm_ref, bas_ref, pl_ref, sel_ref, turn_ref):
    angle = jnp.where(lax.axis_index("seg") == 0, ang_ref[0], F32(0.0))
    angles = jnp.full((8, 128), angle, F32)
    turn_ref[0:8, :] = jnp.cos(angles)
    turn_ref[8:16, :] = jnp.sin(angles)
    _, cvl = corner_parts(cor_ref)
    bm_ref[...] = hot(row_of(cvl) == iota((128, 1), 0).astype(F32))
    bas_ref[...] = lb_ref[:, :NODES]
    columns = slot_columns(fs_ref)
    target = shared_target_row()
    for f in range(FACES):
        pl_ref[f * ELEMS : (f + 1) * ELEMS, :] = hot(columns[f] == target)
    lane = iota((1, 4 * PLANE), 1)
    face, p, q = lane >> 6, (lane >> 3) & 7, lane & 7
    middle = p * PLANE + q + jnp.where(face == 1, 56, 0)
    outer = p * PLANE + q * 8 + jnp.where(face == 3, 7, 0)
    sel_ref[...] = hot(iota((NODES, 1), 0) == jnp.where(face < 2, middle, outer))


def last_kernel(
    tan_ref, s2_ref, sum_ref, across_ref, kh_ref, kl_ref, bm_ref, bas_ref, pl_ref, sel_ref, cor_ref, turn_ref,
    out_ref,
):
    even = (lax.axis_index("dom") & 1) == 0
    near, far = across_ref[8 : 8 + SHARED, :], across_ref[8 + SHARED :, :]
    arrived = jnp.concatenate([jnp.where(even, far, near), jnp.where(even, near, far)], axis=0)
    partly = s2_ref[...] + F32(0.5) * halo_part(pl_ref[...], arrived, sel_ref[...])
    cvh, _ = corner_parts(cor_ref)
    solved = solve(sum_ref[...] + across_ref[0:8, :], kh_ref[...], kl_ref[...])
    state = partly - dot_tn(corner_values(solved, row_of(cvh), bm_ref[...]), bas_ref[...])
    cosine = jnp.concatenate([turn_ref[0:1, :]] * 4, axis=1)
    sine = jnp.concatenate([turn_ref[8:9, :]] * 4, axis=1)
    re, im = state[:ELEMS], state[ELEMS:]
    out_ref[0:ELEMS, :] = tan_ref[0:ELEMS, :] - (cosine * re - sine * im)
    out_ref[ELEMS:, :] = tan_ref[ELEMS:, :] - (sine * re + cosine * im)


VMEM = pl.BlockSpec(memory_space=pltpu.VMEM)
HBM = pl.BlockSpec(memory_space=pltpu.HBM)


def call(body, outs, scratch, ins, flops, specs=None, outs_at=None, limit=28):
    size = sum(int(np.prod(o.shape)) * o.dtype.itemsize for o in outs)
    size += sum(int(np.prod(a.shape)) * a.dtype.itemsize for a in ins)
    return pl.pallas_call(
        body,
        out_shape=outs,
        in_specs=specs or [VMEM] * len(ins),
        out_specs=outs_at or [VMEM] * len(outs),
        scratch_shapes=scratch,
        compiler_params=pltpu.CompilerParams(vmem_limit_bytes=limit * 1024 * 1024),
        cost_estimate=pl.CostEstimate(flops=flops, bytes_accessed=size, transcendentals=0),
    )(*ins)


def like(*shape, dtype=F32):
    return jax.ShapeDtypeStruct(shape, dtype)


def shards(tangent, base_swirl, metric, stiffness, face_slot, corners, coarse_inverse, phase_angle):
    basis, pair, select = tables()
    basis, pair, select = jnp.asarray(basis), jnp.asarray(pair), jnp.asarray(select, dtype=BF16)
    state = tangent.reshape(2 * ELEMS, NODES)
    swirl = base_swirl.reshape(ELEMS, NODES)
    slots = face_slot.T
    ids = corners.T
    field = like(2 * ELEMS, NODES)
    square = like(NODES, NODES, dtype=BF16)
    count = FACES * ELEMS
    faces = pltpu.VMEM((count, 2 * HALO), BF16)

    ins = [state, swirl, metric, stiffness, slots, ids, select, basis, pair, coarse_inverse]
    advanced, g, msg, p, bm, bh, bl, kh, kl, placed, lb = call(
        first_kernel,
        [
            field,
            like(count, 2 * HALO, dtype=BF16),
            like(8, MSG1, 128),
            like(count, count, dtype=BF16),
            like(128, 8 * ELEMS, dtype=BF16),
            square,
            square,
            square,
            square,
            like(count, HALO, dtype=BF16),
            like(32, 2 * NODES, dtype=BF16),
        ],
        [faces]
        + [pltpu.VMEM(a.shape, a.dtype) for a in ins]
        + [pltpu.SemaphoreType.DMA((len(ins),))],
        [pltpu.with_memory_space_constraint(a, pltpu.HBM) for a in ins],
        4_000_000_000,
        [HBM] * len(ins),
    )
    got = lax.all_to_all(msg, "dom", 0, 0)
    s2, msg, near = call(
        second_kernel,
        [field, like(4, 8 + SHARED, 128), like(SHARED, 128)],
        [faces, faces],
        [advanced, g, got, p, bm, bh, bl, kh, kl, placed, lb, swirl, metric, slots, ids, select, basis, pair],
        4_000_000_000,
    )
    size = lax.axis_size("seg")
    ring = [(i, (i + 1) % size) for i in range(size)]

    def onward(target):
        return [(8 * i + d, 8 * j + target(d)) for i, j in ring for d in range(8)]

    s2 = lax.ppermute(s2, "seg", ring)
    got = lax.all_to_all(msg, "dom", 0, 0, axis_index_groups=[[0, 2, 4, 6], [1, 3, 5, 7]])
    total, across = call(pack_kernel, [like(8, 128), like(8 + HALO, 128)], [], [got, near], 1_000_000)
    across = lax.ppermute(across, ("seg", "dom"), onward(lambda d: d ^ 1))
    total = lax.ppermute(total, "seg", ring)
    bm, wide, placed, select, turn = call(
        prepare_kernel,
        [
            like(128, 8 * ELEMS, dtype=BF16),
            like(32, NODES, dtype=BF16),
            like(count, HALO, dtype=BF16),
            like(NODES, 4 * PLANE, dtype=BF16),
            like(16, 128),
        ],
        [],
        [lb, ids, slots, phase_angle],
        1_000_000_000,
        [VMEM] * 3 + [pl.BlockSpec(memory_space=pltpu.SMEM)],
    )
    (out,) = call(
        last_kernel,
        [field],
        [],
        [state, s2, total, across, kh, kl, bm, wide, placed, select, ids, turn],
        1_000_000_000,
    )
    return out.reshape(1, 2, ELEMS, NODES)


def solution(mesh):
    return jax.shard_map(
        shards,
        mesh=mesh,
        in_specs=(
            P("seg", None, "dom", None),
            P("seg", "dom", None),
            P("dom", None),
            P(),
            P("dom", None),
            P("dom", None),
            P(),
            P(),
        ),
        out_specs=P("seg", None, "dom", None),
        check_vma=False,
    )
```

```python
import jax
import jax.numpy as jnp
import numpy as np
from jax import lax
from jax.experimental import pallas as pl
from jax.experimental.pallas import tpu as pltpu
from jax.sharding import PartitionSpec as P

F32 = jnp.float32
BF16 = jnp.bfloat16
NP = 8
NODES = 512
ELEMS = 256
FACES = 6
PLANE = 64
SHARED = 64
HALO = 2 * SHARED
INNER_TOP = 768
MSG1 = 88
FACE_CORNERS = (
    (0, 1, 2, 3),
    (4, 5, 6, 7),
    (0, 1, 4, 5),
    (2, 3, 6, 7),
    (0, 2, 4, 6),
    (1, 3, 5, 7),
)


def tables():
    points = -np.cos(np.pi * np.arange(NP) / (NP - 1))
    linear = np.stack([(1.0 - points) / 2.0, (1.0 + points) / 2.0])
    basis = (
        linear[:, None, None, :, None, None]
        * linear[None, :, None, None, :, None]
        * linear[None, None, :, None, None, :]
    ).reshape(8, NODES)
    flat = (linear[:, None, :, None] * linear[None, :, None, :]).reshape(4, PLANE)
    pair = np.zeros((8, 2 * PLANE))
    pair[:4, :PLANE] = flat
    pair[4:, PLANE:] = flat
    node = np.arange(NODES).reshape(NP, NP, NP)
    faces = [node[:, 0], node[:, -1], node[:, :, 0], node[:, :, -1]]
    chosen = np.concatenate([f.reshape(-1) for f in faces])
    select = (np.arange(NODES)[:, None] == chosen[None, :]).astype(np.float32)
    return basis.astype(np.float32), pair.astype(np.float32), select


def dot(a, b):
    return lax.dot_general(a, b, (((1,), (0,)), ((), ())), preferred_element_type=F32)


def dot_nt(a, b):
    return lax.dot_general(a, b, (((1,), (1,)), ((), ())), preferred_element_type=F32)


def dot_tn(a, b):
    return lax.dot_general(a, b, (((0,), (0,)), ((), ())), preferred_element_type=F32)


def split(x):
    high = x.astype(BF16)
    return high, (x - high.astype(F32)).astype(BF16)


def stacked(x):
    high = x.astype(BF16).astype(F32)
    return jnp.concatenate([high, x - high], axis=0).astype(BF16)


def hot(mask):
    return jnp.where(mask, F32(1.0), F32(0.0)).astype(BF16)


def iota(shape, dim):
    return lax.broadcasted_iota(jnp.int32, shape, dim)


def slot_rows(fs_ref):
    rows = fs_ref[...].astype(F32)
    return [rows[f : f + 1, :] for f in range(FACES)]


def slot_columns(fs_ref):
    rows = fs_ref[...].astype(F32)
    columns = jnp.concatenate([rows, rows[:2]], axis=0).T
    return [columns[:, f : f + 1] for f in range(FACES)]


def corner_parts(cor_ref):
    ids = cor_ref[...]
    return (ids >> 7).astype(F32), (ids & 127).astype(F32)


def row_of(parts):
    return jnp.concatenate([parts[k : k + 1, :] for k in range(parts.shape[0])], axis=1)


def stiff_of(state, bh, bl):
    high, low = split(state)
    return dot(high, bh) + dot(low, bh) + dot(high, bl)


def stiff_matrix(sti):
    rest = sti - sti.astype(BF16).astype(F32)
    low = rest - rest.astype(BF16).astype(F32)
    parts = jnp.concatenate(
        [sti.astype(BF16).astype(F32), rest.astype(BF16).astype(F32), low, jnp.zeros((8, 8), F32)], axis=0
    ).astype(BF16)
    row, col = iota((NODES, 8), 0), iota((NODES, 8), 1)
    col32, lane = iota((32, NODES), 0), iota((32, NODES), 1)
    from_n = iota((NODES, 1), 0)
    to_n = iota((1, NODES), 1)
    total = jnp.zeros((NODES, NODES), F32)
    for shift, keep in ((6, 63), (3, 455), (0, 504)):
        source = hot(((row >> shift) & 7) == col)
        target = hot(((lane >> shift) & 7) == (col32 & 7))
        spread = dot_nt(source, parts)
        spread = dot(spread.astype(BF16), target)
        same = (from_n & keep) == (to_n & keep)
        total = total + jnp.where(same, spread, F32(0.0))
    return total


def advance(state, stiff, metric, swirl):
    re, im = state[:ELEMS], state[ELEMS:]
    new_re = re - metric * stiff[:ELEMS] - swirl * im
    new_im = im - metric * stiff[ELEMS:] + swirl * re
    return jnp.concatenate([new_re, new_im], axis=0)


def face_blocks(advanced, select):
    ah, al = split(advanced)
    fh, fl = dot(ah, select), dot(al, select)
    high, low = ah.astype(F32), al.astype(F32)
    ends = (slice(0, PLANE), slice(NODES - PLANE, NODES))
    pairs = [(high[:, lanes], low[:, lanes]) for lanes in ends]
    for f in range(4):
        lanes = slice(f * PLANE, (f + 1) * PLANE)
        pairs.append((fh[:, lanes], fl[:, lanes]))
    blocks = [
        jnp.concatenate([h[:ELEMS], h[ELEMS:], l[:ELEMS], l[ELEMS:]], axis=1).astype(BF16) for h, l in pairs
    ]
    return blocks, ah, al


def scattered(blocks, select):
    def element_rows(faces, offset):
        re = jnp.concatenate([b[:, offset : offset + PLANE] for b in faces], axis=1)
        im = jnp.concatenate([b[:, offset + PLANE : offset + 2 * PLANE] for b in faces], axis=1)
        return jnp.concatenate([re, im], axis=0)

    high = element_rows(blocks[2:], 0).astype(BF16)
    low = element_rows(blocks[2:], HALO).astype(BF16)
    inner = dot_nt(high, select) + dot_nt(low, select)
    ends = []
    for block in blocks[:2]:
        both = block[:, :HALO] + block[:, HALO:]
        ends.append(jnp.concatenate([both[:, :PLANE], both[:, PLANE:]], axis=0))
    gap = jnp.zeros((2 * ELEMS, NODES - 2 * PLANE), F32)
    return inner + jnp.concatenate([ends[0], gap, ends[1]], axis=1)


def multiplicity():
    n = iota((1, NODES), 1)
    total = jnp.zeros((1, NODES), F32)
    for shift in (6, 3, 0):
        at = (n >> shift) & 7
        total = total + jnp.where((at == 0) | (at == 7), F32(1.0), F32(0.0))
    return total


def deposit(values, high_ids, low_hot):
    vh = (iota((8, 1), 0) & 3).astype(F32)
    chosen = jnp.where(high_ids == vh, values, F32(0.0))
    both = dot_nt(stacked(chosen), low_hot)
    return both[:8] + both[8:]


def eight(re, im):
    return jnp.where(iota((8, 1), 0) < 4, re, im)


def two_products(table, high, low):
    first = dot_nt(stacked(table), high)
    second = dot_nt(stacked(table), low)
    return first[:8] + first[8:] + second[:8]


def coarse_of(ah, al, partner, basis, pair, cvh, bm):
    own = two_products(basis * ((F32(1.0) - F32(0.5) * multiplicity()) * F32(1.0 / NODES)), ah, al)
    lifted = two_products(pair * F32(0.5 / NODES), partner[:, :HALO], partner[:, HALO:])
    values = []
    for k in range(8):
        total = eight(own[k : k + 1, :ELEMS], own[k : k + 1, ELEMS:])
        for f in range(FACES):
            if k in FACE_CORNERS[f]:
                r = FACE_CORNERS[f].index(k)
                lanes = slice(f * ELEMS, (f + 1) * ELEMS)
                total = total + eight(lifted[r : r + 1, lanes], lifted[4 + r : 5 + r, lanes])
        values.append(total)
    return deposit(jnp.concatenate(values, axis=1), row_of(cvh), bm)


def solve(coarse, kh, kl):
    rows = [jnp.concatenate([coarse[4 * c + h : 4 * c + h + 1] for h in range(4)], axis=1) for c in range(2)]
    flat = jnp.concatenate(rows, axis=0)
    high = flat.astype(BF16).astype(F32)
    packed = jnp.concatenate([high, flat - high, jnp.zeros((12, NODES), F32)], axis=0).astype(BF16)
    first = dot_nt(packed, kh)
    second = dot_nt(packed, kl)
    solved = first[0:2] + first[2:4] + second[0:2]
    return jnp.concatenate(
        [solved[c : c + 1, 128 * h : 128 * (h + 1)] for c in range(2) for h in range(4)], axis=0
    )


def corner_values(solved, cvh_row, bm):
    both = dot(stacked(solved), bm)
    spread = both[:8] + both[8:]
    vh = (iota((8, 1), 0) & 3).astype(F32)
    spread = jnp.where(cvh_row == vh, spread, F32(0.0))
    lines = []
    for c in range(2):
        line = jnp.sum(spread[4 * c : 4 * c + 4], axis=0, keepdims=True)
        lines.append(jnp.concatenate([line[:, ELEMS * k : ELEMS * (k + 1)] for k in range(8)], axis=0))
    by_corner = jnp.concatenate(lines, axis=1)
    high = by_corner.astype(BF16).astype(F32)
    return jnp.concatenate([high, by_corner - high, high, jnp.zeros((8, NODES), F32)], axis=0).astype(BF16)


def tripled(table):
    high = table.astype(BF16).astype(F32)
    return jnp.concatenate([high, high, table - high, jnp.zeros_like(high)], axis=0).astype(BF16)


def shared_target_column():
    s = iota((HALO, 1), 0)
    return jnp.where(s < SHARED, s, s + (INNER_TOP - SHARED)).astype(F32)


def shared_target_row():
    s = iota((1, HALO), 1)
    return jnp.where(s < SHARED, s, s + (INNER_TOP - SHARED)).astype(F32)


def halo_faces(placed, arrived):
    high, low = split(arrived)
    both = jnp.concatenate([high.astype(F32), low.astype(F32)], axis=1).astype(BF16)
    return dot(placed, both)


def halo_part(placed, arrived, select):
    got = halo_faces(placed, arrived)
    return scattered([got[f * ELEMS : (f + 1) * ELEMS] for f in range(FACES)], select)


def settle(advanced, partner, select):
    blocks = [partner[f * ELEMS : (f + 1) * ELEMS] for f in range(FACES)]
    kept = advanced * (F32(1.0) - F32(0.5) * multiplicity())
    return kept + F32(0.5) * scattered(blocks, select)


def pair_up(blocks, p_ref, q_ref, g_ref):
    for f in range(FACES):
        q_ref[f * ELEMS : (f + 1) * ELEMS, :] = blocks[f]
    for f in range(FACES):
        rows = slice(f * ELEMS, (f + 1) * ELEMS)
        g_ref[rows, :] = dot(p_ref[rows, :], q_ref[...]).astype(BF16)


def send_rows(msg_ref, me, head, rows):
    count = head.shape[0]
    up, down = rows[:SHARED], rows[SHARED:]
    after = lax.rem(me + 1, 8)
    for j in range(8):
        msg_ref[j, 0:count, :] = head
        msg_ref[j, count : count + SHARED, :] = jnp.where(after == j, down, up)


def first_kernel(
    tan_hbm, swl_hbm, met_hbm, sti_hbm, fs_hbm, cor_hbm, sel_hbm, bas_hbm, pair_hbm, inv_hbm, ang_ref,
    adv_ref, g_ref, msg_ref, p_ref, bm_ref, bh_ref, bl_ref, kh_ref, kl_ref, pl_ref, lb_ref, turn_ref,
    q_ref, tan_ref, swl_ref, met_ref, sti_ref, fs_ref, cor_ref, sel_ref, bas_ref, pair_ref, inv_ref, sems,
):
    me = lax.axis_index("dom")
    moves = [
        pltpu.make_async_copy(src, dst, sems.at[i])
        for i, (src, dst) in enumerate(
            (
                (sti_hbm, sti_ref),
                (fs_hbm, fs_ref),
                (cor_hbm, cor_ref),
                (tan_hbm, tan_ref),
                (met_hbm, met_ref),
                (swl_hbm, swl_ref),
                (sel_hbm, sel_ref),
                (bas_hbm, bas_ref),
                (pair_hbm, pair_ref),
                (inv_hbm, inv_ref),
            )
        )
    ]
    for move in moves:
        move.start()
    angle = jnp.where(lax.axis_index("seg") == 0, ang_ref[0], F32(0.0))
    angles = jnp.full((8, 128), angle, F32)
    turn_ref[0:8, :] = jnp.cos(angles)
    turn_ref[8:16, :] = jnp.sin(angles)
    for move in moves[:3]:
        move.wait()
    bh, bl = split(stiff_matrix(sti_ref[...]))
    bh_ref[...] = bh
    bl_ref[...] = bl
    rows = slot_rows(fs_ref)
    columns = slot_columns(fs_ref)
    other = iota((ELEMS, 1), 0) != iota((1, ELEMS), 1)
    for f in range(FACES):
        for g in range(FACES):
            same = columns[f] == rows[g]
            if f == g:
                same = same & other
            p_ref[f * ELEMS : (f + 1) * ELEMS, g * ELEMS : (g + 1) * ELEMS] = hot(same)
    cvh, cvl = corner_parts(cor_ref)
    bm_ref[...] = hot(row_of(cvl) == iota((128, 1), 0).astype(F32))
    shared = hot(shared_target_column() == jnp.concatenate(rows, axis=1))
    face_ids = jnp.concatenate(
        [
            jnp.concatenate(
                [part[FACE_CORNERS[f][r] : FACE_CORNERS[f][r] + 1, :] for f in range(FACES)], axis=1
            )
            for part in (cvh, cvl)
            for r in range(4)
        ]
        * 2,
        axis=0,
    ).astype(BF16)
    ids = dot_nt(face_ids, shared)[:8]
    target = shared_target_row()
    for f in range(FACES):
        pl_ref[f * ELEMS : (f + 1) * ELEMS, :] = hot(columns[f] == target)
    for move in moves[3:9]:
        move.wait()
    basis = bas_ref[...]
    stiff = stiff_of(jnp.concatenate([basis, basis], axis=0), bh_ref[...], bl_ref[...])
    lb_ref[:, :NODES] = tripled(basis)
    lb_ref[:, NODES:] = tripled(stiff[:8])

    state = tan_ref[...]
    advanced = advance(state, stiff_of(state, bh_ref[...], bl_ref[...]), met_ref[...], swl_ref[...])
    adv_ref[...] = advanced
    blocks, ah, al = face_blocks(advanced, sel_ref[...])
    pair_up(blocks, p_ref, q_ref, g_ref)
    coarse = coarse_of(ah, al, g_ref[...], bas_ref[...], pair_ref[...], cvh, bm_ref[...])
    y = dot(shared, q_ref[...])
    yh, yl = y[:, :HALO], y[:, HALO:]
    rf = two_products(pair_ref[...] * F32(0.5 / NODES), yh.astype(BF16), yl.astype(BF16))
    send_rows(msg_ref, me, jnp.concatenate([coarse, rf, ids], axis=0), yh + yl)
    moves[9].wait()
    kh, kl = split(inv_ref[...])
    kh_ref[...] = kh
    kl_ref[...] = kl


def second_kernel(
    adv_ref, g1_ref, got_ref, p_ref, bm_ref, bh_ref, bl_ref, kh_ref, kl_ref, pl_ref, lb_ref, swl_ref, met_ref, fs_ref, cor_ref,
    sel_ref, bas_ref, pair_ref,
    out_ref, msg_ref, near_ref, q_ref, g_ref,
):
    me = lax.axis_index("dom")
    before, after = lax.rem(me + 7, 8), lax.rem(me + 1, 8)
    select = sel_ref[...]
    cvh, _ = corner_parts(cor_ref)
    cvh_row = row_of(cvh)
    which = iota((128, 1), 0).astype(F32)

    arrived = jnp.concatenate([got_ref[before, 24:MSG1, :], got_ref[after, 24:MSG1, :]], axis=0)
    partner = g1_ref[...].astype(F32) + halo_faces(pl_ref[...], arrived)
    partly = settle(adv_ref[...], partner, select)
    stiff = stiff_of(partly, bh_ref[...], bl_ref[...])

    coarse = got_ref[0, 0:8, :]
    for j in range(1, 8):
        coarse = coarse + got_ref[j, 0:8, :]
    rf = jnp.concatenate([got_ref[j, 8:16, :] for j in range(8)], axis=1)
    ids = jnp.concatenate([got_ref[j, 16:24, :] for j in range(8)], axis=1)
    from_left = jnp.concatenate([ids[:, 1024 - SHARED :], ids[:, : 1024 - SHARED]], axis=1)
    from_right = jnp.concatenate([ids[:, SHARED:], ids[:, :SHARED]], axis=1)
    partner = jnp.where((iota((1, 1024), 1) & SHARED) == 0, from_left, from_right)
    for r in range(4):
        low_hot = hot(partner[4 + r : 5 + r, :] == which)
        coarse = coarse + deposit(
            eight(rf[r : r + 1, :], rf[4 + r : 5 + r, :]), partner[r : r + 1, :], low_hot
        )
    solved = solve(coarse, kh_ref[...], kl_ref[...])
    both = dot_tn(corner_values(solved, cvh_row, bm_ref[...]), lb_ref[...])
    advanced = advance(partly - both[:, :NODES], stiff - both[:, NODES:], met_ref[...], swl_ref[...])
    blocks, ah, al = face_blocks(advanced, select)
    pair_up(blocks, p_ref, q_ref, g_ref)
    out_ref[...] = settle(advanced, g_ref[...].astype(F32), select)
    coarse = coarse_of(ah, al, g_ref[...], bas_ref[...], pair_ref[...], cvh, bm_ref[...])
    shared = hot(shared_target_column() == jnp.concatenate(slot_rows(fs_ref), axis=1))
    y = dot(shared, q_ref[...])
    yh, yl = y[:, :HALO], y[:, HALO:]
    rf = two_products(pair_ref[...] * F32(0.5 / NODES), yh.astype(BF16), yl.astype(BF16))
    mine = jnp.concatenate([got_ref[before, 16:24, SHARED:], got_ref[after, 16:24, :SHARED]], axis=1)
    for r in range(4):
        low_hot = hot(mine[4 + r : 5 + r, :] == which)
        coarse = coarse + deposit(eight(rf[r : r + 1, :], rf[4 + r : 5 + r, :]), mine[r : r + 1, :], low_hot)
    rows = yh + yl
    even = (me & 1) == 0
    near_ref[...] = jnp.where(even, rows[SHARED:], rows[:SHARED])
    far = jnp.where(even, rows[:SHARED], rows[SHARED:])
    for j in range(4):
        msg_ref[j, 0:8, :] = coarse
        msg_ref[j, 8:, :] = far


def pack_kernel(got_ref, near_ref, sum_ref, across_ref):
    me = lax.axis_index("dom")
    coarse = got_ref[0, 0:8, :]
    for j in range(1, 4):
        coarse = coarse + got_ref[j, 0:8, :]
    sum_ref[...] = coarse
    across_ref[0:8, :] = coarse
    across_ref[8 : 8 + SHARED, :] = near_ref[...]
    giver = (me // 2 + jnp.where((me & 1) == 0, 1, 3)) & 3
    across_ref[8 + SHARED :, :] = got_ref[giver, 8:, :]


def prepare_kernel(sum_ref, lb_ref, cor_ref, fs_ref, kept_ref, bm_ref, bas_ref, pl_ref, sel_ref):
    kept_ref[...] = sum_ref[...]
    _, cvl = corner_parts(cor_ref)
    bm_ref[...] = hot(row_of(cvl) == iota((128, 1), 0).astype(F32))
    bas_ref[...] = lb_ref[:, :NODES]
    columns = slot_columns(fs_ref)
    target = shared_target_row()
    for f in range(FACES):
        pl_ref[f * ELEMS : (f + 1) * ELEMS, :] = hot(columns[f] == target)
    lane = iota((1, 4 * PLANE), 1)
    face, p, q = lane >> 6, (lane >> 3) & 7, lane & 7
    middle = p * PLANE + q + jnp.where(face == 1, 56, 0)
    outer = p * PLANE + q * 8 + jnp.where(face == 3, 7, 0)
    sel_ref[...] = hot(iota((NODES, 1), 0) == jnp.where(face < 2, middle, outer))


def last_kernel(
    tan_ref, s2_ref, sum_ref, across_ref, kh_ref, kl_ref, bm_ref, bas_ref, pl_ref, sel_ref, cor_ref, turn_ref,
    out_ref,
):
    even = (lax.axis_index("dom") & 1) == 0
    near, far = across_ref[8 : 8 + SHARED, :], across_ref[8 + SHARED :, :]
    arrived = jnp.concatenate([jnp.where(even, far, near), jnp.where(even, near, far)], axis=0)
    partly = s2_ref[...] + F32(0.5) * halo_part(pl_ref[...], arrived, sel_ref[...])
    cvh, _ = corner_parts(cor_ref)
    solved = solve(sum_ref[...] + across_ref[0:8, :], kh_ref[...], kl_ref[...])
    state = partly - dot_tn(corner_values(solved, row_of(cvh), bm_ref[...]), bas_ref[...])
    cosine = jnp.concatenate([turn_ref[0:1, :]] * 4, axis=1)
    sine = jnp.concatenate([turn_ref[8:9, :]] * 4, axis=1)
    re, im = state[:ELEMS], state[ELEMS:]
    out_ref[0:ELEMS, :] = tan_ref[0:ELEMS, :] - (cosine * re - sine * im)
    out_ref[ELEMS:, :] = tan_ref[ELEMS:, :] - (sine * re + cosine * im)


VMEM = pl.BlockSpec(memory_space=pltpu.VMEM)
HBM = pl.BlockSpec(memory_space=pltpu.HBM)


def call(body, outs, scratch, ins, flops, specs=None, outs_at=None, limit=28):
    size = sum(int(np.prod(o.shape)) * o.dtype.itemsize for o in outs)
    size += sum(int(np.prod(a.shape)) * a.dtype.itemsize for a in ins)
    return pl.pallas_call(
        body,
        out_shape=outs,
        in_specs=specs or [VMEM] * len(ins),
        out_specs=outs_at or [VMEM] * len(outs),
        scratch_shapes=scratch,
        compiler_params=pltpu.CompilerParams(vmem_limit_bytes=limit * 1024 * 1024),
        cost_estimate=pl.CostEstimate(flops=flops, bytes_accessed=size, transcendentals=0),
    )(*ins)


def like(*shape, dtype=F32):
    return jax.ShapeDtypeStruct(shape, dtype)


def shards(tangent, base_swirl, metric, stiffness, face_slot, corners, coarse_inverse, phase_angle):
    basis, pair, select = tables()
    basis, pair, select = jnp.asarray(basis), jnp.asarray(pair), jnp.asarray(select, dtype=BF16)
    state = tangent.reshape(2 * ELEMS, NODES)
    swirl = base_swirl.reshape(ELEMS, NODES)
    slots = face_slot.T
    ids = corners.T
    field = like(2 * ELEMS, NODES)
    square = like(NODES, NODES, dtype=BF16)
    count = FACES * ELEMS
    faces = pltpu.VMEM((count, 2 * HALO), BF16)

    ins = [state, swirl, metric, stiffness, slots, ids, select, basis, pair, coarse_inverse]
    advanced, g, msg, p, bm, bh, bl, kh, kl, placed, lb, turn = call(
        first_kernel,
        [
            field,
            like(count, 2 * HALO, dtype=BF16),
            like(8, MSG1, 128),
            like(count, count, dtype=BF16),
            like(128, 8 * ELEMS, dtype=BF16),
            square,
            square,
            square,
            square,
            like(count, HALO, dtype=BF16),
            like(32, 2 * NODES, dtype=BF16),
            like(16, 128),
        ],
        [faces]
        + [pltpu.VMEM(a.shape, a.dtype) for a in ins]
        + [pltpu.SemaphoreType.DMA((len(ins),))],
        [pltpu.with_memory_space_constraint(a, pltpu.HBM) for a in ins] + [phase_angle],
        4_000_000_000,
        [HBM] * len(ins) + [pl.BlockSpec(memory_space=pltpu.SMEM)],
    )
    got = lax.all_to_all(msg, "dom", 0, 0)
    s2, msg, near = call(
        second_kernel,
        [field, like(4, 8 + SHARED, 128), like(SHARED, 128)],
        [faces, faces],
        [advanced, g, got, p, bm, bh, bl, kh, kl, placed, lb, swirl, metric, slots, ids, select, basis, pair],
        4_000_000_000,
    )
    size = lax.axis_size("seg")
    ring = [(i, (i + 1) % size) for i in range(size)]

    def onward(target):
        return [(8 * i + d, 8 * j + target(d)) for i, j in ring for d in range(8)]

    s2 = lax.ppermute(s2, "seg", ring)
    got = lax.all_to_all(msg, "dom", 0, 0, axis_index_groups=[[0, 2, 4, 6], [1, 3, 5, 7]])
    total, across = call(pack_kernel, [like(8, 128), like(8 + HALO, 128)], [], [got, near], 1_000_000)
    across = lax.ppermute(across, ("seg", "dom"), onward(lambda d: d ^ 1))
    total, bm, wide, placed, select = call(
        prepare_kernel,
        [
            like(8, 128),
            like(128, 8 * ELEMS, dtype=BF16),
            like(32, NODES, dtype=BF16),
            like(count, HALO, dtype=BF16),
            like(NODES, 4 * PLANE, dtype=BF16),
        ],
        [],
        [total, lb, ids, slots],
        1_000_000_000,
    )
    total = lax.ppermute(total, "seg", ring)
    (out,) = call(
        last_kernel,
        [field],
        [],
        [state, s2, total, across, kh, kl, bm, wide, placed, select, ids, turn],
        1_000_000_000,
    )
    return out.reshape(1, 2, ELEMS, NODES)


def solution(mesh):
    return jax.shard_map(
        shards,
        mesh=mesh,
        in_specs=(
            P("seg", None, "dom", None),
            P("seg", "dom", None),
            P("dom", None),
            P(),
            P("dom", None),
            P("dom", None),
            P(),
            P(),
        ),
        out_specs=P("seg", None, "dom", None),
        check_vma=False,
    )
```

```python
import jax
import jax.numpy as jnp
import numpy as np
from jax import lax
from jax.experimental import pallas as pl
from jax.experimental.pallas import tpu as pltpu
from jax.sharding import PartitionSpec as P

F32 = jnp.float32
BF16 = jnp.bfloat16
NP = 8
NODES = 512
ELEMS = 256
FACES = 6
PLANE = 64
SHARED = 64
HALO = 2 * SHARED
INNER_TOP = 768
MSG1 = 88
FACE_CORNERS = (
    (0, 1, 2, 3),
    (4, 5, 6, 7),
    (0, 1, 4, 5),
    (2, 3, 6, 7),
    (0, 2, 4, 6),
    (1, 3, 5, 7),
)


def tables():
    points = -np.cos(np.pi * np.arange(NP) / (NP - 1))
    linear = np.stack([(1.0 - points) / 2.0, (1.0 + points) / 2.0])
    basis = (
        linear[:, None, None, :, None, None]
        * linear[None, :, None, None, :, None]
        * linear[None, None, :, None, None, :]
    ).reshape(8, NODES)
    flat = (linear[:, None, :, None] * linear[None, :, None, :]).reshape(4, PLANE)
    pair = np.zeros((8, 2 * PLANE))
    pair[:4, :PLANE] = flat
    pair[4:, PLANE:] = flat
    node = np.arange(NODES).reshape(NP, NP, NP)
    faces = [node[:, 0], node[:, -1], node[:, :, 0], node[:, :, -1]]
    chosen = np.concatenate([f.reshape(-1) for f in faces])
    select = (np.arange(NODES)[:, None] == chosen[None, :]).astype(np.float32)
    return basis.astype(np.float32), pair.astype(np.float32), select


def dot(a, b):
    return lax.dot_general(a, b, (((1,), (0,)), ((), ())), preferred_element_type=F32)


def dot_nt(a, b):
    return lax.dot_general(a, b, (((1,), (1,)), ((), ())), preferred_element_type=F32)


def dot_tn(a, b):
    return lax.dot_general(a, b, (((0,), (0,)), ((), ())), preferred_element_type=F32)


def split(x):
    high = x.astype(BF16)
    return high, (x - high.astype(F32)).astype(BF16)


def stacked(x):
    high = x.astype(BF16).astype(F32)
    return jnp.concatenate([high, x - high], axis=0).astype(BF16)


def hot(mask):
    return jnp.where(mask, F32(1.0), F32(0.0)).astype(BF16)


def iota(shape, dim):
    return lax.broadcasted_iota(jnp.int32, shape, dim)


def slot_rows(fs_ref):
    rows = fs_ref[...].astype(F32)
    return [rows[f : f + 1, :] for f in range(FACES)]


def slot_columns(fs_ref):
    rows = fs_ref[...].astype(F32)
    columns = jnp.concatenate([rows, rows[:2]], axis=0).T
    return [columns[:, f : f + 1] for f in range(FACES)]


def corner_parts(cor_ref):
    ids = cor_ref[...]
    return (ids >> 7).astype(F32), (ids & 127).astype(F32)


def row_of(parts):
    return jnp.concatenate([parts[k : k + 1, :] for k in range(parts.shape[0])], axis=1)


def stiff_of(state, bh, bl):
    high, low = split(state)
    return dot(high, bh) + dot(low, bh) + dot(high, bl)


def stiff_matrix(sti):
    rest = sti - sti.astype(BF16).astype(F32)
    low = rest - rest.astype(BF16).astype(F32)
    parts = jnp.concatenate(
        [sti.astype(BF16).astype(F32), rest.astype(BF16).astype(F32), low, jnp.zeros((8, 8), F32)], axis=0
    ).astype(BF16)
    row, col = iota((NODES, 8), 0), iota((NODES, 8), 1)
    col32, lane = iota((32, NODES), 0), iota((32, NODES), 1)
    from_n = iota((NODES, 1), 0)
    to_n = iota((1, NODES), 1)
    total = jnp.zeros((NODES, NODES), F32)
    for shift, keep in ((6, 63), (3, 455), (0, 504)):
        source = hot(((row >> shift) & 7) == col)
        target = hot(((lane >> shift) & 7) == (col32 & 7))
        spread = dot_nt(source, parts)
        spread = dot(spread.astype(BF16), target)
        same = (from_n & keep) == (to_n & keep)
        total = total + jnp.where(same, spread, F32(0.0))
    return total


def advance(state, stiff, metric, swirl):
    re, im = state[:ELEMS], state[ELEMS:]
    new_re = re - metric * stiff[:ELEMS] - swirl * im
    new_im = im - metric * stiff[ELEMS:] + swirl * re
    return jnp.concatenate([new_re, new_im], axis=0)


def face_blocks(advanced, select):
    ah, al = split(advanced)
    fh, fl = dot(ah, select), dot(al, select)
    high, low = ah.astype(F32), al.astype(F32)
    ends = (slice(0, PLANE), slice(NODES - PLANE, NODES))
    pairs = [(high[:, lanes], low[:, lanes]) for lanes in ends]
    for f in range(4):
        lanes = slice(f * PLANE, (f + 1) * PLANE)
        pairs.append((fh[:, lanes], fl[:, lanes]))
    blocks = [
        jnp.concatenate([h[:ELEMS], h[ELEMS:], l[:ELEMS], l[ELEMS:]], axis=1).astype(BF16) for h, l in pairs
    ]
    return blocks, ah, al


def scattered(blocks, select):
    def element_rows(faces, offset):
        re = jnp.concatenate([b[:, offset : offset + PLANE] for b in faces], axis=1)
        im = jnp.concatenate([b[:, offset + PLANE : offset + 2 * PLANE] for b in faces], axis=1)
        return jnp.concatenate([re, im], axis=0)

    high = element_rows(blocks[2:], 0).astype(BF16)
    low = element_rows(blocks[2:], HALO).astype(BF16)
    inner = dot_nt(high, select) + dot_nt(low, select)
    ends = []
    for block in blocks[:2]:
        both = block[:, :HALO] + block[:, HALO:]
        ends.append(jnp.concatenate([both[:, :PLANE], both[:, PLANE:]], axis=0))
    gap = jnp.zeros((2 * ELEMS, NODES - 2 * PLANE), F32)
    return inner + jnp.concatenate([ends[0], gap, ends[1]], axis=1)


def multiplicity():
    n = iota((1, NODES), 1)
    total = jnp.zeros((1, NODES), F32)
    for shift in (6, 3, 0):
        at = (n >> shift) & 7
        total = total + jnp.where((at == 0) | (at == 7), F32(1.0), F32(0.0))
    return total


def deposit(values, high_ids, low_hot):
    vh = (iota((8, 1), 0) & 3).astype(F32)
    chosen = jnp.where(high_ids == vh, values, F32(0.0))
    both = dot_nt(stacked(chosen), low_hot)
    return both[:8] + both[8:]


def eight(re, im):
    return jnp.where(iota((8, 1), 0) < 4, re, im)


def two_products(table, high, low):
    first = dot_nt(stacked(table), high)
    second = dot_nt(stacked(table), low)
    return first[:8] + first[8:] + second[:8]


def coarse_of(ah, al, partner, basis, pair, cvh, bm):
    own = two_products(basis * ((F32(1.0) - F32(0.5) * multiplicity()) * F32(1.0 / NODES)), ah, al)
    lifted = two_products(pair * F32(0.5 / NODES), partner[:, :HALO], partner[:, HALO:])
    values = []
    for k in range(8):
        total = eight(own[k : k + 1, :ELEMS], own[k : k + 1, ELEMS:])
        for f in range(FACES):
            if k in FACE_CORNERS[f]:
                r = FACE_CORNERS[f].index(k)
                lanes = slice(f * ELEMS, (f + 1) * ELEMS)
                total = total + eight(lifted[r : r + 1, lanes], lifted[4 + r : 5 + r, lanes])
        values.append(total)
    return deposit(jnp.concatenate(values, axis=1), row_of(cvh), bm)


def solve(coarse, kh, kl):
    rows = [jnp.concatenate([coarse[4 * c + h : 4 * c + h + 1] for h in range(4)], axis=1) for c in range(2)]
    flat = jnp.concatenate(rows, axis=0)
    high = flat.astype(BF16).astype(F32)
    packed = jnp.concatenate([high, flat - high, jnp.zeros((12, NODES), F32)], axis=0).astype(BF16)
    first = dot_nt(packed, kh)
    second = dot_nt(packed, kl)
    solved = first[0:2] + first[2:4] + second[0:2]
    return jnp.concatenate(
        [solved[c : c + 1, 128 * h : 128 * (h + 1)] for c in range(2) for h in range(4)], axis=0
    )


def corner_values(solved, cvh_row, bm):
    both = dot(stacked(solved), bm)
    spread = both[:8] + both[8:]
    vh = (iota((8, 1), 0) & 3).astype(F32)
    spread = jnp.where(cvh_row == vh, spread, F32(0.0))
    lines = []
    for c in range(2):
        line = jnp.sum(spread[4 * c : 4 * c + 4], axis=0, keepdims=True)
        lines.append(jnp.concatenate([line[:, ELEMS * k : ELEMS * (k + 1)] for k in range(8)], axis=0))
    by_corner = jnp.concatenate(lines, axis=1)
    high = by_corner.astype(BF16).astype(F32)
    return jnp.concatenate([high, by_corner - high, high, jnp.zeros((8, NODES), F32)], axis=0).astype(BF16)


def tripled(table):
    high = table.astype(BF16).astype(F32)
    return jnp.concatenate([high, high, table - high, jnp.zeros_like(high)], axis=0).astype(BF16)


def shared_target_column():
    s = iota((HALO, 1), 0)
    return jnp.where(s < SHARED, s, s + (INNER_TOP - SHARED)).astype(F32)


def shared_target_row():
    s = iota((1, HALO), 1)
    return jnp.where(s < SHARED, s, s + (INNER_TOP - SHARED)).astype(F32)


def halo_faces(placed, arrived):
    high, low = split(arrived)
    both = jnp.concatenate([high.astype(F32), low.astype(F32)], axis=1).astype(BF16)
    return dot(placed, both)


def halo_part(placed, arrived, select):
    got = halo_faces(placed, arrived)
    return scattered([got[f * ELEMS : (f + 1) * ELEMS] for f in range(FACES)], select)


def settle(advanced, partner, select):
    blocks = [partner[f * ELEMS : (f + 1) * ELEMS] for f in range(FACES)]
    kept = advanced * (F32(1.0) - F32(0.5) * multiplicity())
    return kept + F32(0.5) * scattered(blocks, select)


def pair_up(blocks, p_ref, q_ref, g_ref):
    for f in range(FACES):
        q_ref[f * ELEMS : (f + 1) * ELEMS, :] = blocks[f]
    for f in range(FACES):
        rows = slice(f * ELEMS, (f + 1) * ELEMS)
        g_ref[rows, :] = dot(p_ref[rows, :], q_ref[...]).astype(BF16)


def send_rows(msg_ref, me, head, rows):
    count = head.shape[0]
    up, down = rows[:SHARED], rows[SHARED:]
    after = lax.rem(me + 1, 8)
    for j in range(8):
        msg_ref[j, 0:count, :] = head
        msg_ref[j, count : count + SHARED, :] = jnp.where(after == j, down, up)


def first_kernel(
    tan_hbm, swl_hbm, met_hbm, sti_hbm, fs_hbm, cor_hbm, sel_hbm, bas_hbm, pair_hbm, inv_hbm, ang_ref,
    adv_ref, g_ref, msg_ref, p_ref, bm_ref, bh_ref, bl_ref, kh_ref, kl_ref, pl_ref, turn_ref,
    q_ref, tan_ref, swl_ref, met_ref, sti_ref, fs_ref, cor_ref, sel_ref, bas_ref, pair_ref, inv_ref, sems,
):
    me = lax.axis_index("dom")
    moves = [
        pltpu.make_async_copy(src, dst, sems.at[i])
        for i, (src, dst) in enumerate(
            (
                (sti_hbm, sti_ref),
                (fs_hbm, fs_ref),
                (cor_hbm, cor_ref),
                (tan_hbm, tan_ref),
                (met_hbm, met_ref),
                (swl_hbm, swl_ref),
                (sel_hbm, sel_ref),
                (bas_hbm, bas_ref),
                (pair_hbm, pair_ref),
                (inv_hbm, inv_ref),
            )
        )
    ]
    for move in moves:
        move.start()
    angle = jnp.where(lax.axis_index("seg") == 0, ang_ref[0], F32(0.0))
    angles = jnp.full((8, 128), angle, F32)
    turn_ref[0:8, :] = jnp.cos(angles)
    turn_ref[8:16, :] = jnp.sin(angles)
    for move in moves[:3]:
        move.wait()
    bh, bl = split(stiff_matrix(sti_ref[...]))
    bh_ref[...] = bh
    bl_ref[...] = bl
    rows = slot_rows(fs_ref)
    columns = slot_columns(fs_ref)
    other = iota((ELEMS, 1), 0) != iota((1, ELEMS), 1)
    for f in range(FACES):
        for g in range(FACES):
            same = columns[f] == rows[g]
            if f == g:
                same = same & other
            p_ref[f * ELEMS : (f + 1) * ELEMS, g * ELEMS : (g + 1) * ELEMS] = hot(same)
    cvh, cvl = corner_parts(cor_ref)
    bm_ref[...] = hot(row_of(cvl) == iota((128, 1), 0).astype(F32))
    shared = hot(shared_target_column() == jnp.concatenate(rows, axis=1))
    face_ids = jnp.concatenate(
        [
            jnp.concatenate(
                [part[FACE_CORNERS[f][r] : FACE_CORNERS[f][r] + 1, :] for f in range(FACES)], axis=1
            )
            for part in (cvh, cvl)
            for r in range(4)
        ]
        * 2,
        axis=0,
    ).astype(BF16)
    ids = dot_nt(face_ids, shared)[:8]
    target = shared_target_row()
    for f in range(FACES):
        pl_ref[f * ELEMS : (f + 1) * ELEMS, :] = hot(columns[f] == target)
    for move in moves[3:9]:
        move.wait()

    state = tan_ref[...]
    advanced = advance(state, stiff_of(state, bh_ref[...], bl_ref[...]), met_ref[...], swl_ref[...])
    adv_ref[...] = advanced
    blocks, ah, al = face_blocks(advanced, sel_ref[...])
    pair_up(blocks, p_ref, q_ref, g_ref)
    coarse = coarse_of(ah, al, g_ref[...], bas_ref[...], pair_ref[...], cvh, bm_ref[...])
    y = dot(shared, q_ref[...])
    yh, yl = y[:, :HALO], y[:, HALO:]
    rf = two_products(pair_ref[...] * F32(0.5 / NODES), yh.astype(BF16), yl.astype(BF16))
    send_rows(msg_ref, me, jnp.concatenate([coarse, rf, ids], axis=0), yh + yl)
    moves[9].wait()
    kh, kl = split(inv_ref[...])
    kh_ref[...] = kh
    kl_ref[...] = kl


def second_kernel(
    adv_ref, g1_ref, got_ref, p_ref, bm_ref, bh_ref, bl_ref, kh_ref, kl_ref, pl_ref, swl_ref, met_ref, fs_ref, cor_ref,
    sel_ref, bas_ref, pair_ref,
    out_ref, msg_ref, near_ref, q_ref, g_ref,
):
    me = lax.axis_index("dom")
    before, after = lax.rem(me + 7, 8), lax.rem(me + 1, 8)
    select = sel_ref[...]
    cvh, _ = corner_parts(cor_ref)
    cvh_row = row_of(cvh)
    which = iota((128, 1), 0).astype(F32)

    arrived = jnp.concatenate([got_ref[before, 24:MSG1, :], got_ref[after, 24:MSG1, :]], axis=0)
    partner = g1_ref[...].astype(F32) + halo_faces(pl_ref[...], arrived)
    partly = settle(adv_ref[...], partner, select)
    basis = bas_ref[...]
    stiff = stiff_of(jnp.concatenate([partly, basis, basis], axis=0), bh_ref[...], bl_ref[...])
    wide = jnp.concatenate([tripled(basis), tripled(stiff[2 * ELEMS : 2 * ELEMS + 8])], axis=1)
    stiff = stiff[: 2 * ELEMS]

    coarse = got_ref[0, 0:8, :]
    for j in range(1, 8):
        coarse = coarse + got_ref[j, 0:8, :]
    rf = jnp.concatenate([got_ref[j, 8:16, :] for j in range(8)], axis=1)
    ids = jnp.concatenate([got_ref[j, 16:24, :] for j in range(8)], axis=1)
    from_left = jnp.concatenate([ids[:, 1024 - SHARED :], ids[:, : 1024 - SHARED]], axis=1)
    from_right = jnp.concatenate([ids[:, SHARED:], ids[:, :SHARED]], axis=1)
    partner = jnp.where((iota((1, 1024), 1) & SHARED) == 0, from_left, from_right)
    for r in range(4):
        low_hot = hot(partner[4 + r : 5 + r, :] == which)
        coarse = coarse + deposit(
            eight(rf[r : r + 1, :], rf[4 + r : 5 + r, :]), partner[r : r + 1, :], low_hot
        )
    solved = solve(coarse, kh_ref[...], kl_ref[...])
    both = dot_tn(corner_values(solved, cvh_row, bm_ref[...]), wide)
    advanced = advance(partly - both[:, :NODES], stiff - both[:, NODES:], met_ref[...], swl_ref[...])
    blocks, ah, al = face_blocks(advanced, select)
    pair_up(blocks, p_ref, q_ref, g_ref)
    out_ref[...] = settle(advanced, g_ref[...].astype(F32), select)
    coarse = coarse_of(ah, al, g_ref[...], bas_ref[...], pair_ref[...], cvh, bm_ref[...])
    shared = hot(shared_target_column() == jnp.concatenate(slot_rows(fs_ref), axis=1))
    y = dot(shared, q_ref[...])
    yh, yl = y[:, :HALO], y[:, HALO:]
    rf = two_products(pair_ref[...] * F32(0.5 / NODES), yh.astype(BF16), yl.astype(BF16))
    mine = jnp.concatenate([got_ref[before, 16:24, SHARED:], got_ref[after, 16:24, :SHARED]], axis=1)
    for r in range(4):
        low_hot = hot(mine[4 + r : 5 + r, :] == which)
        coarse = coarse + deposit(eight(rf[r : r + 1, :], rf[4 + r : 5 + r, :]), mine[r : r + 1, :], low_hot)
    rows = yh + yl
    even = (me & 1) == 0
    near_ref[...] = jnp.where(even, rows[SHARED:], rows[:SHARED])
    far = jnp.where(even, rows[:SHARED], rows[SHARED:])
    for j in range(4):
        msg_ref[j, 0:8, :] = coarse
        msg_ref[j, 8:, :] = far


def pack_kernel(got_ref, near_ref, sum_ref, across_ref):
    me = lax.axis_index("dom")
    coarse = got_ref[0, 0:8, :]
    for j in range(1, 4):
        coarse = coarse + got_ref[j, 0:8, :]
    sum_ref[...] = coarse
    across_ref[0:8, :] = coarse
    across_ref[8 : 8 + SHARED, :] = near_ref[...]
    giver = (me // 2 + jnp.where((me & 1) == 0, 1, 3)) & 3
    across_ref[8 + SHARED :, :] = got_ref[giver, 8:, :]


def prepare_kernel(sum_ref, basis_ref, cor_ref, fs_ref, kept_ref, bm_ref, bas_ref, pl_ref, sel_ref):
    kept_ref[...] = sum_ref[...]
    _, cvl = corner_parts(cor_ref)
    bm_ref[...] = hot(row_of(cvl) == iota((128, 1), 0).astype(F32))
    bas_ref[...] = tripled(basis_ref[...])
    columns = slot_columns(fs_ref)
    target = shared_target_row()
    for f in range(FACES):
        pl_ref[f * ELEMS : (f + 1) * ELEMS, :] = hot(columns[f] == target)
    lane = iota((1, 4 * PLANE), 1)
    face, p, q = lane >> 6, (lane >> 3) & 7, lane & 7
    middle = p * PLANE + q + jnp.where(face == 1, 56, 0)
    outer = p * PLANE + q * 8 + jnp.where(face == 3, 7, 0)
    sel_ref[...] = hot(iota((NODES, 1), 0) == jnp.where(face < 2, middle, outer))


def last_kernel(
    tan_ref, s2_ref, sum_ref, across_ref, kh_ref, kl_ref, bm_ref, bas_ref, pl_ref, sel_ref, cor_ref, turn_ref,
    out_ref,
):
    even = (lax.axis_index("dom") & 1) == 0
    near, far = across_ref[8 : 8 + SHARED, :], across_ref[8 + SHARED :, :]
    arrived = jnp.concatenate([jnp.where(even, far, near), jnp.where(even, near, far)], axis=0)
    partly = s2_ref[...] + F32(0.5) * halo_part(pl_ref[...], arrived, sel_ref[...])
    cvh, _ = corner_parts(cor_ref)
    solved = solve(sum_ref[...] + across_ref[0:8, :], kh_ref[...], kl_ref[...])
    state = partly - dot_tn(corner_values(solved, row_of(cvh), bm_ref[...]), bas_ref[...])
    cosine = jnp.concatenate([turn_ref[0:1, :]] * 4, axis=1)
    sine = jnp.concatenate([turn_ref[8:9, :]] * 4, axis=1)
    re, im = state[:ELEMS], state[ELEMS:]
    out_ref[0:ELEMS, :] = tan_ref[0:ELEMS, :] - (cosine * re - sine * im)
    out_ref[ELEMS:, :] = tan_ref[ELEMS:, :] - (sine * re + cosine * im)


VMEM = pl.BlockSpec(memory_space=pltpu.VMEM)
HBM = pl.BlockSpec(memory_space=pltpu.HBM)


def call(body, outs, scratch, ins, flops, specs=None, outs_at=None, limit=28):
    size = sum(int(np.prod(o.shape)) * o.dtype.itemsize for o in outs)
    size += sum(int(np.prod(a.shape)) * a.dtype.itemsize for a in ins)
    return pl.pallas_call(
        body,
        out_shape=outs,
        in_specs=specs or [VMEM] * len(ins),
        out_specs=outs_at or [VMEM] * len(outs),
        scratch_shapes=scratch,
        compiler_params=pltpu.CompilerParams(vmem_limit_bytes=limit * 1024 * 1024),
        cost_estimate=pl.CostEstimate(flops=flops, bytes_accessed=size, transcendentals=0),
    )(*ins)


def like(*shape, dtype=F32):
    return jax.ShapeDtypeStruct(shape, dtype)


def shards(tangent, base_swirl, metric, stiffness, face_slot, corners, coarse_inverse, phase_angle):
    basis, pair, select = tables()
    basis, pair, select = jnp.asarray(basis), jnp.asarray(pair), jnp.asarray(select, dtype=BF16)
    state = tangent.reshape(2 * ELEMS, NODES)
    swirl = base_swirl.reshape(ELEMS, NODES)
    slots = face_slot.T
    ids = corners.T
    field = like(2 * ELEMS, NODES)
    square = like(NODES, NODES, dtype=BF16)
    count = FACES * ELEMS
    faces = pltpu.VMEM((count, 2 * HALO), BF16)

    ins = [state, swirl, metric, stiffness, slots, ids, select, basis, pair, coarse_inverse]
    advanced, g, msg, p, bm, bh, bl, kh, kl, placed, turn = call(
        first_kernel,
        [
            field,
            like(count, 2 * HALO, dtype=BF16),
            like(8, MSG1, 128),
            like(count, count, dtype=BF16),
            like(128, 8 * ELEMS, dtype=BF16),
            square,
            square,
            square,
            square,
            like(count, HALO, dtype=BF16),
            like(16, 128),
        ],
        [faces]
        + [pltpu.VMEM(a.shape, a.dtype) for a in ins]
        + [pltpu.SemaphoreType.DMA((len(ins),))],
        [pltpu.with_memory_space_constraint(a, pltpu.HBM) for a in ins] + [phase_angle],
        4_000_000_000,
        [HBM] * len(ins) + [pl.BlockSpec(memory_space=pltpu.SMEM)],
    )
    got = lax.all_to_all(msg, "dom", 0, 0)
    s2, msg, near = call(
        second_kernel,
        [field, like(4, 8 + SHARED, 128), like(SHARED, 128)],
        [faces, faces],
        [advanced, g, got, p, bm, bh, bl, kh, kl, placed, swirl, metric, slots, ids, select, basis, pair],
        4_000_000_000,
    )
    size = lax.axis_size("seg")
    ring = [(i, (i + 1) % size) for i in range(size)]

    def onward(target):
        return [(8 * i + d, 8 * j + target(d)) for i, j in ring for d in range(8)]

    s2 = lax.ppermute(s2, "seg", ring)
    got = lax.all_to_all(msg, "dom", 0, 0, axis_index_groups=[[0, 2, 4, 6], [1, 3, 5, 7]])
    total, across = call(pack_kernel, [like(8, 128), like(8 + HALO, 128)], [], [got, near], 1_000_000)
    across = lax.ppermute(across, ("seg", "dom"), onward(lambda d: d ^ 1))
    total, bm, wide, placed, select = call(
        prepare_kernel,
        [
            like(8, 128),
            like(128, 8 * ELEMS, dtype=BF16),
            like(32, NODES, dtype=BF16),
            like(count, HALO, dtype=BF16),
            like(NODES, 4 * PLANE, dtype=BF16),
        ],
        [],
        [total, basis, ids, slots],
        1_000_000_000,
    )
    total = lax.ppermute(total, "seg", ring)
    (out,) = call(
        last_kernel,
        [field],
        [],
        [state, s2, total, across, kh, kl, bm, wide, placed, select, ids, turn],
        1_000_000_000,
    )
    return out.reshape(1, 2, ELEMS, NODES)


def solution(mesh):
    return jax.shard_map(
        shards,
        mesh=mesh,
        in_specs=(
            P("seg", None, "dom", None),
            P("seg", "dom", None),
            P("dom", None),
            P(),
            P("dom", None),
            P("dom", None),
            P(),
            P(),
        ),
        out_specs=P("seg", None, "dom", None),
        check_vma=False,
    )
```
